256 devices in a mesh: gx: 8 (over y, x_lo), gy: 16 (over x_hi, z), gz: 2 (over core).
Axes of the slice: x: 4 (x_hi: 2, x_lo: 2; x = x_hi * 2 + x_lo), y: 4, z: 8, core: 2. Of those that a mesh axis runs over, the one named last changes fastest.
Arguments:
- charges: bfloat16 [8, 16, 2, 16, 2048], P('gx', 'gy', 'gz'), may hold values from -6 to 6
- positions: float32 [8, 16, 2, 3, 2048], P('gx', 'gy', 'gz'), may hold values from -0.5 to 0.5
- atom_cells: int32 [8, 16, 2, 2048], P('gx', 'gy', 'gz'), may hold values from 0 to 216, never falling along the last dimension, each value on 1 to 32 neighbouring positions
- offsets: int32 [2, 128, 3], replicated, may hold values from -3 to 3, as said below
- far_tables: bfloat16 [2, 49, 49, 128], replicated, may hold values from -0.01953125 to 0.01953125
- upward_tables: bfloat16 [8, 49, 49], replicated, may hold values from -0.3125 to 0.3125
- downward_tables: bfloat16 [8, 49, 49], replicated, may hold values from -0.875 to 0.875
Outputs:
- potential: float32 [8, 16, 2, 16, 2048], P('gx', 'gy', 'gz')
The draws below stay inside these ranges and needn't reach their ends.
Inputs may be any that keep to these rules, and one draw needn't show every extreme that they name: `atom_cells`: within each device block the entries never fall along the slots; the value 216 marks padding slots, which come last; every cell and the padding hold 1 to 32 slots. For each level the 128 offsets are distinct, the largest magnitude of each offset's coordinates is 2 to 3, and the six offsets of 3 cells along a single axis are always among them.
All inputs are finite; a program needn't handle non-finite values.
Results may differ from the reference program's by a relative error of at most 0.0041.
Values may be sent and summed in bfloat16 or wider, within the bound.
No kernel may reach another device: no remote copies, remote signals or barrier semaphores. Data moves between devices by JAX's collectives and lax.ppermute only.
A program may use at most 128 MiB of HBM per device.

```python
import math
import jax
import jax.numpy as jnp
import numpy as np
from jax import lax

CH = 16
ORDER = 6
TERMS = 49
REACH = 3
NOFF = 128
CX = 6
CY = 6
CZ = 6
CELL_MOST = 32
ATOMS_DEV = 2048
CELLS = 216
BLOCKS_X = 8
BLOCKS_Y = 16
BLOCKS_Z = 2
NX = 48
NY = 96
NZ = 12


def draw_offsets(key, part):
    key = jax.random.fold_in(key, 11)
    values_line = np.arange(-REACH, REACH + 1)
    lattice = np.stack(np.meshgrid(values_line, values_line, values_line, indexing='ij'), -1).reshape(-1, 3)
    reach_of = np.max(np.abs(lattice), axis=1)
    nonzero_count = np.sum(lattice != 0, axis=1)
    axial_mask = (reach_of == REACH) & (nonzero_count == 1)
    remote_mask = (reach_of >= 2) & ~axial_mask
    axial_rows = jnp.asarray(lattice[axial_mask], jnp.int32)
    remote_rows = jnp.asarray(lattice[remote_mask], jnp.int32)
    levels_out = []
    for level_id in range(2):
        level_key = jax.random.fold_in(key, level_id)
        picked = jax.random.permutation(level_key, remote_rows.shape[0])[:NOFF - 6]
        chosen = jnp.concatenate([axial_rows, remote_rows[picked]], axis=0)
        mixing = jax.random.permutation(jax.random.fold_in(level_key, 5), NOFF)
        levels_out.append(chosen[mixing])
    return jnp.stack(levels_out, 0).astype(jnp.int32)


def block_scale(rng, dims, split, least, largest):
    def one(dim, parts):
        steps = jax.random.uniform(jax.random.fold_in(jax.random.fold_in(rng, 6), dim), (parts,), jnp.float32, least / len(split), largest / len(split))
        return jnp.repeat(jnp.exp(steps), dims[dim] // parts).reshape((-1,) + (1,) * (len(dims) - dim - 1))

    factor_of = one(*split[0])
    for cut in split[1:]:
        factor_of = factor_of * one(*cut)
    return factor_of


def profile(amount, total, most, lean):
    weights = [(1 << 20) // math.isqrt(grade ** lean) + 1 for grade in range(2, amount + 1)]
    spare, given = total - most - (amount - 1), [1] * (amount - 1)
    while spare > 0:
        movable = [i for i in range(amount - 1) if given[i] < most]
        mass, remaining = sum([weights[i] for i in movable]), spare
        for i in movable:
            more = min(most - given[i], max(1, remaining * weights[i] // mass), spare)
            given[i] = given[i] + more
            spare = spare - more
    return np.array([most] + given)


def ragged(own_key, number_of, total, most, skew):
    if number_of == 2:
        one = jax.random.randint(own_key, (), max(1, total - most), min(most, total - 1) + 1)
        return jnp.stack([one, total - one])
    lengths = jnp.asarray(profile(number_of, total, most, skew), jnp.int32)
    pairs = (number_of - 1) // 2
    giver, sink = lengths[1:1 + 2 * pairs:2], lengths[2:2 + 2 * pairs:2]
    room = jnp.minimum(giver - 1, most - sink)
    moved = jax.random.randint(jax.random.fold_in(own_key, 1), (pairs,), 0, 1 << 20) % (room + 1)
    lengths = lengths.at[1:1 + 2 * pairs:2].set(giver - moved).at[2:2 + 2 * pairs:2].set(sink + moved)
    return lengths[jax.random.permutation(jax.random.fold_in(own_key, 2), number_of)]


def centred(key, extent, scale, bound, pieces=(), dtype=jnp.bfloat16):
    level = block_scale(key, extent, pieces, -0.22, 0.18) if pieces else 1.0
    drawn = jax.random.normal(key, extent, jnp.float32) * scale * level
    return jnp.minimum(jnp.maximum(drawn, -bound), bound).astype(dtype)


def setup_inputs(seed: int = 0) -> dict:
    keys = jax.random.split(jax.random.key(seed), 8)
    charges = centred(keys[0], (BLOCKS_X, BLOCKS_Y, BLOCKS_Z, CH, ATOMS_DEV), 1.0, 6.0, ((0, 8), (1, 16), (2, 2)))
    positions = jnp.clip(jax.random.uniform(keys[1], (BLOCKS_X, BLOCKS_Y, BLOCKS_Z, 3, ATOMS_DEV), jnp.float32, -0.5, 0.5) * block_scale(keys[1], (BLOCKS_X, BLOCKS_Y, BLOCKS_Z, 3, ATOMS_DEV), ((0, 8), (1, 16), (2, 2)), -0.4, 0.0), -0.5, 0.5)
    atom_cells = jax.vmap(lambda own: jnp.searchsorted(jnp.cumsum(ragged(own, CELLS + 1, ATOMS_DEV, CELL_MOST, 1)), jnp.arange(ATOMS_DEV), side="right"))(jax.random.split(keys[2], BLOCKS_X * BLOCKS_Y * BLOCKS_Z)).reshape((BLOCKS_X, BLOCKS_Y, BLOCKS_Z, ATOMS_DEV)).astype(jnp.int32)
    offsets = draw_offsets(jax.random.fold_in(keys[7], 71), 0)
    far_tables = centred(keys[4], (2, TERMS, TERMS, NOFF), (16 * NOFF * TERMS) ** -0.5, 0.01953125)
    upward_tables = centred(keys[5], (8, TERMS, TERMS), (8 * TERMS) ** -0.5, 0.3125)
    downward_tables = centred(keys[6], (8, TERMS, TERMS), TERMS ** -0.5, 0.875)
    return {"charges": charges, "positions": positions, "atom_cells": atom_cells, "offsets": offsets, "far_tables": far_tables, "upward_tables": upward_tables, "downward_tables": downward_tables}


radial_scale = 1.6

def solid_harmonics(coords):
    x_part = coords[0]
    y_part = coords[1]
    z_part = coords[2]
    radius_sq = x_part * x_part + y_part * y_part + z_part * z_part
    zeros_row = jnp.zeros_like(x_part)
    cosines = {(0, 0): jnp.ones_like(x_part)}
    sines = {(0, 0): zeros_row}
    for degree in range(1, ORDER + 1):
        for order_m in range(degree):
            lower_c = cosines[degree - 1, order_m]
            lower_s = sines[degree - 1, order_m]
            if order_m <= degree - 2:
                second_c = cosines[degree - 2, order_m]
                second_s = sines[degree - 2, order_m]
            else:
                second_c = zeros_row
                second_s = zeros_row
            divisor = float((degree + order_m) * (degree - order_m))
            cosines[degree, order_m] = ((2 * degree - 1) * z_part * lower_c - radius_sq * second_c) / divisor
            sines[degree, order_m] = ((2 * degree - 1) * z_part * lower_s - radius_sq * second_s) / divisor
        prev_c = cosines[degree - 1, degree - 1]
        prev_s = sines[degree - 1, degree - 1]
        cosines[degree, degree] = -(x_part * prev_c - y_part * prev_s) / (2.0 * degree)
        sines[degree, degree] = -(x_part * prev_s + y_part * prev_c) / (2.0 * degree)
    terms_list = []
    for degree in range(ORDER + 1):
        terms_list.append(cosines[degree, 0] * float(math.factorial(degree)))
        for order_m in range(1, degree + 1):
            factor = math.sqrt(math.factorial(degree + order_m) * math.factorial(degree - order_m))
            terms_list.append(cosines[degree, order_m] * factor)
            terms_list.append(sines[degree, order_m] * factor)
    return jnp.stack(terms_list, 0)

def block_poles(packed):
    charge_block, place_block, cell_block = packed
    harmonics = solid_harmonics(radial_scale * place_block)
    products = charge_block.astype(jnp.float32).T[:, :, None] * harmonics.T[:, None, :]
    summed = jax.ops.segment_sum(products.reshape(ATOMS_DEV, CH * TERMS), cell_block, num_segments=CELLS)
    return summed.astype(jnp.bfloat16)

def far_field(field_grid, level_tables, level_offsets):
    start_total = jnp.zeros(field_grid.shape, jnp.float32)
    wide_grid = field_grid.astype(jnp.float32)

    def add_offset(offset_id, running):
        offset_now = level_offsets[offset_id]
        shifted = jnp.roll(wide_grid, (-offset_now[0], -offset_now[1], -offset_now[2]), axis=(0, 1, 2))
        table_now = level_tables[:, :, offset_id].astype(jnp.float32)
        return running + jnp.einsum('xyzck,jk->xyzcj', shifted, table_now)
    return lax.fori_loop(0, NOFF, add_offset, start_total)

def reference(charges, positions, atom_cells, offsets, far_tables, upward_tables, downward_tables):
    block_count = BLOCKS_X * BLOCKS_Y * BLOCKS_Z
    charge_flat = charges.reshape(block_count, CH, ATOMS_DEV)
    place_flat = positions.reshape(block_count, 3, ATOMS_DEV)
    cell_flat = atom_cells.reshape(block_count, ATOMS_DEV)
    leaf_blocks = lax.map(block_poles, (charge_flat, place_flat, cell_flat))
    leaf_grid = leaf_blocks.reshape(BLOCKS_X, BLOCKS_Y, BLOCKS_Z, CX, CY, CZ, CH, TERMS)
    leaf_grid = leaf_grid.transpose(0, 3, 1, 4, 2, 5, 6, 7).reshape(NX, NY, NZ, CH, TERMS)
    leaf_grid = lax.optimization_barrier(leaf_grid)
    upward = upward_tables.astype(jnp.float32).reshape(2, 2, 2, TERMS, TERMS)
    children = leaf_grid.astype(jnp.float32).reshape(NX // 2, 2, NY // 2, 2, NZ // 2, 2, CH, TERMS)
    parent_grid = jnp.einsum('xaybzcqk,abcjk->xyzqj', children, upward).astype(jnp.bfloat16)
    parent_grid = lax.optimization_barrier(parent_grid)
    leaf_far = far_field(leaf_grid, far_tables[0], offsets[0])
    parent_far = far_field(parent_grid, far_tables[1], offsets[1]).astype(jnp.bfloat16)
    parent_far = lax.optimization_barrier(parent_far)
    downward = downward_tables.astype(jnp.float32).reshape(2, 2, 2, TERMS, TERMS)
    lifted = jnp.einsum('xyzqk,abcjk->xaybzcqj', parent_far.astype(jnp.float32), downward)
    leaf_locals = leaf_far + lifted.reshape(NX, NY, NZ, CH, TERMS)
    local_blocks = leaf_locals.reshape(BLOCKS_X, CX, BLOCKS_Y, CY, BLOCKS_Z, CZ, CH * TERMS)
    local_blocks = local_blocks.transpose(0, 2, 4, 1, 3, 5, 6).reshape(block_count, CELLS, CH * TERMS)
    padded = jnp.concatenate([local_blocks, jnp.zeros((block_count, 1, CH * TERMS), jnp.float32)], axis=1)

    def block_potential(packed):
        local_table, place_block, cell_block = packed
        harmonics = solid_harmonics(radial_scale * place_block)
        local_rows = local_table[cell_block].reshape(ATOMS_DEV, CH, TERMS)
        return lax.optimization_barrier(jnp.sum(local_rows * harmonics.T[:, None, :], axis=2)).T
    potential = lax.map(block_potential, (padded, place_flat, cell_flat))
    return potential.reshape(BLOCKS_X, BLOCKS_Y, BLOCKS_Z, CH, ATOMS_DEV)
```

```python
import math

import numpy as np
import jax
import jax.numpy as jnp
from jax import lax
from jax.experimental import pallas as pl
from jax.experimental.pallas import tpu as pltpu
from jax.sharding import PartitionSpec as P

CH = 16
ORDER = 6
TERMS = 49
NOFF = 128
SLOTS = 3
PSLOTS = 2
F32 = jnp.float32
BF16 = jnp.bfloat16
NT = (((1,), (1,)), ((), ()))
TN = (((0,), (0,)), ((), ()))
radial_scale = 1.6
MIB = 1 << 20


def spectral_constants():
    leaf_freq = [[None, 2, 4], [1, 3, 5]]
    pair_freq = [[2, 0], [1, 3]]
    turn = 2 * math.pi / 12
    pturn = 2 * math.pi / 6

    def fwd(core, s, ri, z):
        f = leaf_freq[core][s]
        if f is None:
            return float(z % 2 == ri)
        return math.cos(turn * f * z) if ri == 0 else -math.sin(turn * f * z)

    def inv(core, s, ri, z):
        f = leaf_freq[core][s]
        if f is None:
            return float(z % 2 == ri) / 6
        return (math.cos(turn * f * z) if ri == 0 else -math.sin(turn * f * z)) / 6

    def pfwd(core, s, ri, z):
        f = pair_freq[core][s]
        if s == 1:
            return math.cos(pturn * f * z) if ri == 0 else 0.0
        return math.cos(pturn * f * z) if ri == 0 else -math.sin(pturn * f * z)

    def pinv(core, s, ri, z):
        return pfwd(core, s, ri, z) / (6 if s == 1 else 3)

    halves = np.zeros((2, 104, 128))
    for core in range(2):
        row = 0

        def put(a, b):
            nonlocal row
            halves[core, row, :64] = a
            halves[core, row, 64:] = b
            row += 1

        for s in range(SLOTS):
            for v in range(6):
                z = (core if v < 3 else 1 - core) * 6 + 2 * (v % 3)
                put(fwd(core, s, 0, z), fwd(core, s, 1, z + 1))
                put(fwd(core, s, 0, z + 1), fwd(core, s, 1, z))
        for p in range(3):
            z = core * 6 + 2 * p
            for u in range(6):
                own = core if u < 3 else 1 - core
                s = u % 3
                put(inv(own, s, 0, z), inv(own, s, 1, z + 1))
                put(inv(own, s, 1, z), inv(own, s, 0, z + 1))
        for s in range(PSLOTS):
            for v in range(4):
                z = (core if v < 2 else 1 - core) * 3 + 2 * (v % 2)
                on = float(v % 2 == 0)
                put(pfwd(core, s, 0, z), on * pfwd(core, s, 1, z + 1))
                put(on * pfwd(core, s, 0, z + 1), pfwd(core, s, 1, z))
        for p in range(2):
            z = core * 3 + 2 * p
            on = float(p == 0)
            for u in range(4):
                own = core if u < 2 else 1 - core
                s = u % 2
                put(pinv(own, s, 0, z), on * pinv(own, s, 1, z + 1))
                put(pinv(own, s, 1, z), on * pinv(own, s, 0, z + 1))
        assert row == 104
    table = np.zeros((2, 80))
    for core in range(2):
        for pq in range(2):
            for s in range(SLOTS):
                f = leaf_freq[core][s]
                for d in range(7):
                    dz = d - 3
                    if f is None:
                        val = float(dz % 2 == pq)
                    else:
                        val = math.sin(turn * f * dz) if pq else math.cos(turn * f * dz)
                    table[core, (pq * SLOTS + s) * 7 + d] = val
            for s in range(PSLOTS):
                f = pair_freq[core][s]
                for d in range(7):
                    dz = d - 3
                    if s == 1:
                        val = 0.0 if pq else math.cos(pturn * f * dz)
                    else:
                        val = math.sin(pturn * f * dz) if pq else math.cos(pturn * f * dz)
                    table[core, 42 + (pq * PSLOTS + s) * 7 + d] = val
        table[core, 70] = 1.0 if core == 0 else -1.0
    return halves.astype(np.float32), table.reshape(-1).astype(np.float32)


COEFS, ZTABLE = spectral_constants()


def harmonic_terms(x, y, z):
    rsq = x * x + y * y + z * z
    cosines = {(0, 0): jnp.ones_like(x)}
    sines = {}
    for deg in range(1, ORDER + 1):
        for m in range(deg):
            inv = 1.0 / float((deg + m) * (deg - m))
            for part in (cosines, sines):
                if part is sines and m == 0:
                    continue
                val = ((2 * deg - 1) * inv) * (z * part[deg - 1, m])
                if m <= deg - 2:
                    val = val - inv * (rsq * part[deg - 2, m])
                part[deg, m] = val
        scale = -1.0 / (2.0 * deg)
        pc = cosines[deg - 1, deg - 1]
        if deg == 1:
            cosines[1, 1] = scale * x
            sines[1, 1] = scale * y
        else:
            ps = sines[deg - 1, deg - 1]
            cosines[deg, deg] = scale * (x * pc - y * ps)
            sines[deg, deg] = scale * (x * ps + y * pc)
    out = []
    for deg in range(ORDER + 1):
        out.append(cosines[deg, 0] * float(math.factorial(deg)))
        for m in range(1, deg + 1):
            factor = math.sqrt(math.factorial(deg + m) * math.factorial(deg - m))
            out.append(cosines[deg, m] * factor)
            out.append(sines[deg, m] * factor)
    return out


def low_lanes(rows):
    return lax.broadcasted_iota(jnp.int32, (rows, 128), 1) < 64


def cell_number_rows():
    row = lax.broadcasted_iota(jnp.int32, (240, 128), 0)
    z = jnp.zeros_like(row)
    for i in range(1, 6):
        z = z + (row >= 40 * i).astype(jnp.int32)
    xy = row - 40 * z
    return jnp.where(xy < 36, xy * 6 + z, -1)


def poles_kernel(ch_ref, pos_ref, cell_ref, up_ref, zs_ref, h_ref, pos_s, h3_s, chf_s, whi_s, wlo_s, one_s, f_s):
    for d in range(3):
        for i in range(16):
            pos_s[d * 16 + i : d * 16 + i + 1, :] = pos_ref[0, 0, 0, d : d + 1, i * 128 : (i + 1) * 128]
    terms = harmonic_terms(
        radial_scale * pos_s[0:16, :], radial_scale * pos_s[16:32, :], radial_scale * pos_s[32:48, :]
    )
    for k in range(TERMS):
        h3_s[k * 16 : (k + 1) * 16, :] = terms[k]
    h3_s[TERMS * 16 : 1024, :] = jnp.zeros((1024 - TERMS * 16, 128), F32)
    for i in range(16):
        h_ref[:, i * 128 : (i + 1) * 128] = h3_s[pl.ds(i, 64, stride=16), :]
    chf_s[...] = ch_ref[0, 0, 0].astype(F32)
    number = cell_number_rows()
    for i in range(16):
        sl = slice(i * 128, (i + 1) * 128)
        cells = cell_ref[0, 0, :, sl]
        one_s[:, sl] = jnp.where(number == cells, 1.0, 0.0).astype(BF16)
    for c in range(CH):
        for i in range(4):
            sl = slice(i * 512, (i + 1) * 512)
            w = h_ref[:, sl] * chf_s[c : c + 1, sl]
            hi = w.astype(BF16)
            whi_s[c * 64 : (c + 1) * 64, sl] = hi
            wlo_s[c * 64 : (c + 1) * 64, sl] = (w - hi.astype(F32)).astype(BF16)
    low = low_lanes(40)
    for n in range(4):
        rows = slice(n * 256, (n + 1) * 256)
        r = lax.dot_general(one_s[...], whi_s[rows, :], NT, preferred_element_type=F32)
        r = r + lax.dot_general(one_s[...], wlo_s[rows, :], NT, preferred_element_type=F32)
        for half in range(2):
            c = n * 4 + half * 2
            for zp in range(3):
                a = r[zp * 80 : zp * 80 + 40, half * 128 : half * 128 + 128]
                b = r[zp * 80 + 40 : zp * 80 + 80, half * 128 : half * 128 + 128]
                f_s[zp, pl.ds(c, 40, stride=16), :] = jnp.where(low, a, pltpu.roll(b, 64, 1))
                f_s[zp, pl.ds(c + 1, 40, stride=16), :] = jnp.where(low, pltpu.roll(a, 64, 1), b)
    res = []
    for zp in range(3):
        leaf = f_s[zp, 0:576, :].astype(BF16)
        zs_ref[zp * 576 : (zp + 1) * 576, :] = leaf
        split = leaf.reshape(3, 2, 3, 2, 16, 128)
        lhs = jnp.concatenate(
            [split[:, p, :, q].reshape(144, 128) for p in range(2) for q in range(2)], axis=1
        )
        res.append(lax.dot_general(lhs, up_ref[...], NT, preferred_element_type=F32))
    low = low_lanes(144)
    zs_ref[1728:1872, :] = jnp.where(low, res[0], res[1]).astype(BF16)
    zs_ref[1872:2016, :] = jnp.where(low, res[2], 0.0).astype(BF16)


def combine(values, coef, row):
    total = None
    for v, val in enumerate(values):
        part = val * coef(row + 2 * v) + pltpu.roll(val, 64, 1) * coef(row + 2 * v + 1)
        total = part if total is None else total + part
    return total


def forward_kernel(own_ref, other_ref, coef_ref, sl_ref, sr_ref):
    core = lax.axis_index("gz")

    def coef(row):
        return coef_ref[core, row : row + 1, :]

    for x in range(6):
        face = sl_ref if x < 3 else sr_ref
        for y in range(6):
            at = (x * 6 + y) * 16
            values = [
                ref[zp * 576 + at : zp * 576 + at + 16, :].astype(F32)
                for ref in (own_ref, other_ref)
                for zp in range(3)
            ]
            for s in range(SLOTS):
                row = (((s * 3 + x % 3) * 2 + y % 2) * 3 + y // 2) * 16
                face[row : row + 16, :] = combine(values, coef, s * 12).astype(BF16)
    for x in range(3):
        for y in range(3):
            at = 1728 + (x * 3 + y) * 16
            values = [
                ref[at + v * 144 : at + v * 144 + 16, :].astype(F32)
                for ref in (own_ref, other_ref)
                for v in range(2)
            ]
            for s in range(PSLOTS):
                row = 864 + ((s * 3 + x) * 3 + (0, 2, 1)[y]) * 16
                done = combine(values, coef, 72 + s * 8).astype(BF16)
                sl_ref[row : row + 16, :] = done
                sr_ref[row : row + 16, :] = done


def table_kernel(off_ref, zt_ref, far_ref, wl_ref, wp_ref, t3_s, w_s, a_s):
    core = lax.axis_index("gz")
    base = core * 80
    t3_s[...] = jnp.zeros_like(t3_s)
    for level, slots, out_ref, start in ((0, SLOTS, wl_ref, 0), (1, PSLOTS, wp_ref, 42)):
        for j in range(TERMS):
            t3_s[j * 56 : j * 56 + TERMS, :] = far_ref[level, j].astype(F32)
        ox = off_ref[level, 0:1, :]
        oy = off_ref[level, 1:2, :]
        oz = off_ref[level, 2:3, :]
        code = (ox + 3) * 7 + (oy + 3)
        chosen = lax.broadcasted_iota(jnp.int32, (56, 128), 0) == code
        for q in range(2 * slots):
            row = jnp.zeros((1, 128), F32)
            for d in range(7):
                row = jnp.where(oz == d - 3, zt_ref[base + start + q * 7 + d], row)
            full = jnp.where(chosen, row, 0.0)
            hi = full.astype(BF16).astype(F32)
            a_s[q * 56 : (q + 1) * 56, 0:128] = hi
            a_s[q * 56 : (q + 1) * 56, 128:256] = full - hi
        coefs = a_s[0 : 2 * slots * 56, :].astype(BF16)
        count = slots * 56
        low = low_lanes(count)
        block = lax.broadcasted_iota(jnp.int32, (count, 128), 0)
        if level == 0:
            sign = jnp.where(block < 56, zt_ref[base + 70], -1.0)
        else:
            sign = jnp.full((count, 128), -1.0, F32)

        def one_term(k, carry):
            tk = t3_s[pl.ds(k, 64, stride=56), :].astype(BF16)
            wide = jnp.concatenate([tk, tk], axis=1)
            rhs = jnp.concatenate([wide, wide], axis=0)
            out = lax.dot_general(coefs, rhs, NT, preferred_element_type=F32)
            even = out[0:count]
            odd = out[count : 2 * count]
            w_s[pl.ds(k, count, stride=128), :] = jnp.where(low, even, odd)
            w_s[pl.ds(k + 64, count, stride=128), :] = jnp.where(low, sign * odd, even)
            return carry

        lax.fori_loop(0, TERMS, one_term, 0, unroll=7)
        inner = lax.broadcasted_iota(jnp.int32, (128, 128), 0)
        filled = (inner < TERMS) | ((inner >= 64) & (inner < 64 + TERMS))

        def one_block(b, carry):
            val = w_s[pl.ds(pl.multiple_of(b * 128, 128), 128), :]
            out_ref[b] = jnp.where(filled, val, 0.0).astype(BF16)
            return carry

        lax.fori_loop(0, count, one_block, 0, unroll=4)


def far_kernel(a_ref, sl_ref, sr_ref, b_ref, wl_ref, wp_ref, dn_ref, up_ref, own_ref, fl_s, fp_s):
    for i, ref in enumerate((a_ref, sl_ref, sr_ref, b_ref)):
        fl_s[:, 3 * i : 3 * i + 3] = ref[0:864, :].reshape(SLOTS, 3, 2, 48, 128)
    fp_s[...] = jnp.zeros_like(fp_s)
    for i, ref in enumerate((a_ref, sl_ref, b_ref)):
        part = ref[864:1152, :].reshape(PSLOTS, 3, 48, 128)
        fp_s[:, 3 * i : 3 * i + 3, 0] = part[:, :, 0:32]
        fp_s[:, 3 * i : 3 * i + 3, 1, 0:16] = part[:, :, 32:48]

    def level(field, weights, slots, xs, pairs, ys, send_at, own_at):
        spots = ys // 2 if ys % 2 == 0 else ys // 2 + 1
        rows = xs * spots * 16
        zero = jnp.zeros((128, 128), BF16)
        for s in range(slots):

            def weight(xi, dy):
                if dy < -3 or dy > 3:
                    return zero
                return weights[s * 56 + xi * 7 + dy + 3]

            accs = []
            lhs = jnp.concatenate(
                [field[s, xi : xi + xs, p].reshape(rows, 128) for xi in range(7) for p in range(2)],
                axis=1,
            )
            for diff in range(-3, 1):
                d = 2 * diff + 3
                rhs = jnp.concatenate(
                    [
                        jnp.concatenate([weight(xi, d + p), weight(xi, d + p - 1)], axis=1)
                        for xi in range(7)
                        for p in range(2)
                    ],
                    axis=0,
                )
                acc = jnp.dot(lhs, rhs, preferred_element_type=F32)
                accs.append(acc.reshape(xs, spots, 16, 256))
            for pair in range(pairs):
                for o in range(2):
                    yo = 2 * pair - 3 + o
                    if yo >= ys + 3:
                        continue
                    val = None
                    for diff in range(-3, 1):
                        ysp = pair + diff
                        if 0 <= ysp < spots:
                            part = accs[diff + 3][:, ysp, :, o * 128 : (o + 1) * 128]
                            val = part if val is None else val + part
                    for x in range(xs):
                        if yo < 0:
                            at = send_at + ((s * xs + x) * 3 + yo + 3) * 16
                            dn_ref[at : at + 16, :] = val[x].astype(BF16)
                        elif yo < ys:
                            at = own_at + ((s * xs + x) * ys + yo) * 16
                            own_ref[at : at + 16, :] = val[x]
                        else:
                            at = send_at + ((s * xs + x) * 3 + yo - ys) * 16
                            up_ref[at : at + 16, :] = val[x].astype(BF16)

    level(fl_s, wl_ref, SLOTS, 6, 6, 6, 0, 0)
    level(fp_s, wp_ref, PSLOTS, 3, 5, 3, 864, 1728)


def join_kernel(own_ref, from_up_ref, from_dn_ref, full_ref, zs_ref):
    for i in range(18):
        for ref, at in ((from_up_ref, 0), (from_dn_ref, 48)):
            rows = slice(i * 96 + at, i * 96 + at + 48)
            total = own_ref[rows, :] + ref[i * 48 : (i + 1) * 48, :].astype(F32)
            full_ref[rows, :] = total
            zs_ref[rows, :] = total.astype(BF16)
    for i in range(6):
        rows = slice(1728 + i * 48, 1776 + i * 48)
        far = slice(864 + i * 48, 912 + i * 48)
        total = own_ref[rows, :] + from_up_ref[far, :].astype(F32) + from_dn_ref[far, :].astype(F32)
        full_ref[rows, :] = total
        zs_ref[rows, :] = total.astype(BF16)


def atoms_kernel(own_ref, other_ref, coef_ref, cell_ref, h_ref, down_ref, out_ref, pf_s, lift_s, l_s, l2_s, l3_s):
    core = lax.axis_index("gz")

    def coef(row):
        return coef_ref[core, row : row + 1, :]

    for i in range(9):
        at = 1728 + i * 16
        values = [
            ref[at + s * 144 : at + s * 144 + 16, :].astype(F32)
            for ref in (own_ref, other_ref)
            for s in range(PSLOTS)
        ]
        for p in range(2):
            pf_s[p, i * 16 : (i + 1) * 16, :] = combine(values, coef, 88 + p * 8).astype(BF16)
    for k in range(3):
        lift_s[k] = lax.dot_general(pf_s[k // 2], down_ref[k % 2], NT, preferred_element_type=F32)
    for x in range(6):
        for y in range(6):
            at = (x * 6 + y) * 16
            values = [
                ref[s * 576 + at : s * 576 + at + 16, :].astype(F32)
                for ref in (own_ref, other_ref)
                for s in range(SLOTS)
            ]
            par = ((x // 2) * 3 + y // 2) * 16
            lane = ((x % 2) * 2 + y % 2) * 128
            for zp in range(3):
                l_s[zp, at : at + 16, :] = (
                    combine(values, coef, 36 + zp * 12) + lift_s[zp, par : par + 16, lane : lane + 128]
                )
    low = low_lanes(40)
    for zp in range(3):
        l_s[zp, 576:640, :] = jnp.zeros((64, 128), F32)
        for cp in range(8):
            a = l_s[zp, pl.ds(2 * cp, 40, stride=16), :]
            b = l_s[zp, pl.ds(2 * cp + 1, 40, stride=16), :]
            first = jnp.where(low, a, pltpu.roll(b, 64, 1))
            second = jnp.where(low, pltpu.roll(a, 64, 1), b)
            for z, val in ((2 * zp, first), (2 * zp + 1, second)):
                hi = val.astype(BF16).astype(F32)
                l2_s[z * 40 : (z + 1) * 40, cp * 128 : (cp + 1) * 128] = hi
                l3_s[z * 40 : (z + 1) * 40, cp * 128 : (cp + 1) * 128] = val - hi
    high_rows = l2_s[...].T.astype(BF16)
    low_rows = l3_s[...].T.astype(BF16)
    number = cell_number_rows()
    for i in range(8):
        one = []
        for half in range(2):
            cells = cell_ref[0, 0, :, i * 256 + half * 128 : i * 256 + half * 128 + 128]
            one.append(jnp.where(number == cells, 1.0, 0.0).astype(BF16))
        one = jnp.concatenate(one, axis=1)
        spread = jnp.dot(high_rows, one, preferred_element_type=F32)
        spread = spread + jnp.dot(low_rows, one, preferred_element_type=F32)
        spread = spread.reshape(CH, 64, 256)[:, 0:56] * h_ref[0:56, i * 256 : (i + 1) * 256][None]
        out_ref[0, 0, 0, :, i * 256 : (i + 1) * 256] = jnp.sum(spread, axis=1)


def call(kernel, outs, scratch, flops=0, moved=0):
    return pl.pallas_call(
        kernel,
        out_shape=outs,
        scratch_shapes=scratch,
        compiler_params=pltpu.CompilerParams(vmem_limit_bytes=48 * MIB),
        cost_estimate=pl.CostEstimate(flops=flops, bytes_accessed=moved, transcendentals=0),
    )


def shape(dims, dtype):
    return jax.ShapeDtypeStruct(dims, dtype)


def ring(axis):
    count = lax.axis_size(axis)
    forward = [(i, (i + 1) % count) for i in range(count)]
    backward = [(target, source) for source, target in forward]
    return forward, backward


def per_device(charges, positions, atom_cells, offsets, far_tables, upward_tables, downward_tables):
    up = jnp.pad(upward_tables, ((0, 0), (0, 15), (0, 15))).transpose(1, 0, 2).reshape(64, 512)
    up = jnp.concatenate([up, up], axis=0)
    down = jnp.pad(downward_tables, ((0, 0), (0, 15), (0, 15))).reshape(512, 64)
    blank = jnp.zeros_like(down)
    down = jnp.stack(
        [jnp.concatenate([down, blank], axis=1), jnp.concatenate([blank, down], axis=1)], axis=0
    )
    off = offsets.transpose(0, 2, 1)
    coefs = jnp.asarray(COEFS)
    swap = [(0, 1), (1, 0)]

    zs, harm = call(
        poles_kernel,
        (shape((2016, 128), BF16), shape((64, 2048), F32)),
        [
            pltpu.VMEM((48, 128), F32),
            pltpu.VMEM((1024, 128), F32),
            pltpu.VMEM((16, 2048), F32),
            pltpu.VMEM((1024, 2048), BF16),
            pltpu.VMEM((1024, 2048), BF16),
            pltpu.VMEM((240, 2048), BF16),
            pltpu.VMEM((3, 640, 128), F32),
        ],
        2 * 2 * 256 * 2048 * 1024,
        2 * MIB,
    )(charges, positions, atom_cells, up)
    zother = lax.ppermute(zs, "gz", swap)
    wl, wp = pl.pallas_call(
        table_kernel,
        out_shape=(shape((168, 128, 128), BF16), shape((112, 128, 128), BF16)),
        in_specs=[
            pl.BlockSpec(memory_space=pltpu.VMEM),
            pl.BlockSpec(memory_space=pltpu.SMEM),
            pl.BlockSpec(memory_space=pltpu.VMEM),
        ],
        scratch_shapes=[
            pltpu.VMEM((64 * 56, 128), F32),
            pltpu.VMEM((168 * 128, 128), F32),
            pltpu.VMEM((336, 256), F32),
        ],
        compiler_params=pltpu.CompilerParams(vmem_limit_bytes=48 * MIB),
        cost_estimate=pl.CostEstimate(
            flops=2 * 49 * 560 * 256 * 256, bytes_accessed=20 * MIB, transcendentals=0
        ),
    )(off, jnp.asarray(ZTABLE), far_tables)
    sl, sr = call(
        forward_kernel, (shape((1152, 128), BF16), shape((1152, 128), BF16)), [], 0, 2 * MIB
    )(zs, zother, coefs)
    forward, backward = ring("gx")
    from_left = lax.ppermute(sr, "gx", forward)
    from_right = lax.ppermute(sl, "gx", backward)
    dn, ups, own = call(
        far_kernel,
        (shape((1152, 128), BF16), shape((1152, 128), BF16), shape((2016, 128), F32)),
        [pltpu.VMEM((SLOTS, 12, 2, 48, 128), BF16), pltpu.VMEM((PSLOTS, 9, 2, 32, 128), BF16)],
        2 * 288 * 1792 * 256 * 20,
        14 * MIB,
    )(from_left, sl, sr, from_right, wl, wp)
    forward, backward = ring("gy")
    from_above = lax.ppermute(dn, "gy", backward)
    from_below = lax.ppermute(ups, "gy", forward)
    full, zsend = call(
        join_kernel, (shape((2016, 128), F32), shape((2016, 128), BF16)), [], 0, 3 * MIB
    )(own, from_below, from_above)
    zrecv = lax.ppermute(zsend, "gz", swap)
    potential = call(
        atoms_kernel,
        shape((1, 1, 1, CH, 2048), F32),
        [
            pltpu.VMEM((2, 144, 128), BF16),
            pltpu.VMEM((3, 144, 512), F32),
            pltpu.VMEM((3, 640, 128), F32),
            pltpu.VMEM((240, 1024), F32),
            pltpu.VMEM((240, 1024), F32),
        ],
        2 * 2 * 256 * 2048 * 1024,
        2 * MIB,
    )(full, zrecv, coefs, atom_cells, harm, down)
    return potential


def solution(mesh):
    placed = (
        P("gx", "gy", "gz", None, None),
        P("gx", "gy", "gz", None, None),
        P("gx", "gy", "gz", None),
        P(),
        P(),
        P(),
        P(),
    )
    return jax.shard_map(
        per_device,
        mesh=mesh,
        in_specs=placed,
        out_specs=P("gx", "gy", "gz", None, None),
        check_vma=False,
    )
```

```python
import math

import numpy as np
import jax
import jax.numpy as jnp
from jax import lax
from jax.experimental import pallas as pl
from jax.experimental.pallas import tpu as pltpu
from jax.sharding import PartitionSpec as P

CH = 16
ORDER = 6
TERMS = 49
NOFF = 128
SLOTS = 3
PSLOTS = 2
F32 = jnp.float32
BF16 = jnp.bfloat16
NT = (((1,), (1,)), ((), ()))
TN = (((0,), (0,)), ((), ()))
radial_scale = 1.6
MIB = 1 << 20


def spectral_constants():
    leaf_freq = [[None, 2, 4], [1, 3, 5]]
    pair_freq = [[2, 0], [1, 3]]
    turn = 2 * math.pi / 12
    pturn = 2 * math.pi / 6

    def fwd(core, s, ri, z):
        f = leaf_freq[core][s]
        if f is None:
            return float(z % 2 == ri)
        return math.cos(turn * f * z) if ri == 0 else -math.sin(turn * f * z)

    def inv(core, s, ri, z):
        f = leaf_freq[core][s]
        if f is None:
            return float(z % 2 == ri) / 6
        return (math.cos(turn * f * z) if ri == 0 else -math.sin(turn * f * z)) / 6

    def pfwd(core, s, ri, z):
        f = pair_freq[core][s]
        if s == 1:
            return math.cos(pturn * f * z) if ri == 0 else 0.0
        return math.cos(pturn * f * z) if ri == 0 else -math.sin(pturn * f * z)

    def pinv(core, s, ri, z):
        return pfwd(core, s, ri, z) / (6 if s == 1 else 3)

    halves = np.zeros((2, 104, 128))
    for core in range(2):
        row = 0

        def put(a, b):
            nonlocal row
            halves[core, row, :64] = a
            halves[core, row, 64:] = b
            row += 1

        for s in range(SLOTS):
            for v in range(6):
                z = (core if v < 3 else 1 - core) * 6 + 2 * (v % 3)
                put(fwd(core, s, 0, z), fwd(core, s, 1, z + 1))
                put(fwd(core, s, 0, z + 1), fwd(core, s, 1, z))
        for p in range(3):
            z = core * 6 + 2 * p
            for u in range(6):
                own = core if u < 3 else 1 - core
                s = u % 3
                put(inv(own, s, 0, z), inv(own, s, 1, z + 1))
                put(inv(own, s, 1, z), inv(own, s, 0, z + 1))
        for s in range(PSLOTS):
            for v in range(4):
                z = (core if v < 2 else 1 - core) * 3 + 2 * (v % 2)
                on = float(v % 2 == 0)
                put(pfwd(core, s, 0, z), on * pfwd(core, s, 1, z + 1))
                put(on * pfwd(core, s, 0, z + 1), pfwd(core, s, 1, z))
        for p in range(2):
            z = core * 3 + 2 * p
            on = float(p == 0)
            for u in range(4):
                own = core if u < 2 else 1 - core
                s = u % 2
                put(pinv(own, s, 0, z), on * pinv(own, s, 1, z + 1))
                put(pinv(own, s, 1, z), on * pinv(own, s, 0, z + 1))
        assert row == 104
    table = np.zeros((2, 80))
    for core in range(2):
        for pq in range(2):
            for s in range(SLOTS):
                f = leaf_freq[core][s]
                for d in range(7):
                    dz = d - 3
                    if f is None:
                        val = float(dz % 2 == pq)
                    else:
                        val = math.sin(turn * f * dz) if pq else math.cos(turn * f * dz)
                    table[core, (pq * SLOTS + s) * 7 + d] = val
            for s in range(PSLOTS):
                f = pair_freq[core][s]
                for d in range(7):
                    dz = d - 3
                    if s == 1:
                        val = 0.0 if pq else math.cos(pturn * f * dz)
                    else:
                        val = math.sin(pturn * f * dz) if pq else math.cos(pturn * f * dz)
                    table[core, 42 + (pq * PSLOTS + s) * 7 + d] = val
        table[core, 70] = 1.0 if core == 0 else -1.0
    return halves.astype(np.float32), table.reshape(-1).astype(np.float32)


COEFS, ZTABLE = spectral_constants()


def harmonic_terms(x, y, z):
    rsq = x * x + y * y + z * z
    cosines = {(0, 0): jnp.ones_like(x)}
    sines = {}
    for deg in range(1, ORDER + 1):
        for m in range(deg):
            inv = 1.0 / float((deg + m) * (deg - m))
            for part in (cosines, sines):
                if part is sines and m == 0:
                    continue
                val = ((2 * deg - 1) * inv) * (z * part[deg - 1, m])
                if m <= deg - 2:
                    val = val - inv * (rsq * part[deg - 2, m])
                part[deg, m] = val
        scale = -1.0 / (2.0 * deg)
        pc = cosines[deg - 1, deg - 1]
        if deg == 1:
            cosines[1, 1] = scale * x
            sines[1, 1] = scale * y
        else:
            ps = sines[deg - 1, deg - 1]
            cosines[deg, deg] = scale * (x * pc - y * ps)
            sines[deg, deg] = scale * (x * ps + y * pc)
    out = []
    for deg in range(ORDER + 1):
        out.append(cosines[deg, 0] * float(math.factorial(deg)))
        for m in range(1, deg + 1):
            factor = math.sqrt(math.factorial(deg + m) * math.factorial(deg - m))
            out.append(cosines[deg, m] * factor)
            out.append(sines[deg, m] * factor)
    return out


def low_lanes(rows):
    return lax.broadcasted_iota(jnp.int32, (rows, 128), 1) < 64


def cell_number_rows():
    row = lax.broadcasted_iota(jnp.int32, (240, 128), 0)
    z = jnp.zeros_like(row)
    for i in range(1, 6):
        z = z + (row >= 40 * i).astype(jnp.int32)
    xy = row - 40 * z
    return jnp.where(xy < 36, xy * 6 + z, -1)


def start_copies(pairs, sems):
    copies = [pltpu.make_async_copy(src, dst, sems.at[i]) for i, (src, dst) in enumerate(pairs)]
    for copy in copies:
        copy.start()
    return copies


def fill_harmonics(pos_s, h3_s, h_ref):
    terms = harmonic_terms(
        radial_scale * pos_s[0:16, :], radial_scale * pos_s[16:32, :], radial_scale * pos_s[32:48, :]
    )
    for k in range(TERMS):
        h3_s[k * 16 : (k + 1) * 16, :] = terms[k]
    h3_s[TERMS * 16 : 1024, :] = jnp.zeros((1024 - TERMS * 16, 128), F32)
    for i in range(16):
        h_ref[:, i * 128 : (i + 1) * 128] = h3_s[pl.ds(i, 64, stride=16), :]


def fill_onehot(cell_s, one_ref):
    number = cell_number_rows()
    for i in range(16):
        one_ref[:, i * 128 : (i + 1) * 128] = jnp.where(number == cell_s[i : i + 1, :], 1.0, 0.0).astype(BF16)


def atom_terms_kernel(pos_ref, cell_ref, h_ref, one_ref, h3_s):
    fill_harmonics(pos_ref, h3_s, h_ref)
    fill_onehot(cell_ref, one_ref)


def poles_kernel(ch_hbm, pos_hbm, cell_hbm, zs_ref, h_s, one_s, ch_s, pos_s, cell_s, h3_s, chf_s, whi_s, wlo_s, rt_s, f_s, sems):
    copies = start_copies(((pos_hbm, pos_s), (cell_hbm, cell_s), (ch_hbm.at[0, 0, 0], ch_s)), sems)
    copies[0].wait()
    fill_harmonics(pos_s, h3_s, h_s)
    copies[1].wait()
    fill_onehot(cell_s, one_s)
    copies[2].wait()
    chf_s[...] = ch_s[...].astype(F32)
    for c in range(CH):
        for i in range(4):
            sl = slice(i * 512, (i + 1) * 512)
            w = h_s[:, sl] * chf_s[c : c + 1, sl]
            hi = w.astype(BF16)
            whi_s[c * 64 : (c + 1) * 64, sl] = hi
            wlo_s[c * 64 : (c + 1) * 64, sl] = (w - hi.astype(F32)).astype(BF16)
    low = low_lanes(40)
    rt_s[...] = lax.dot_general(whi_s[...], one_s[...], NT, preferred_element_type=F32) + lax.dot_general(
        wlo_s[...], one_s[...], NT, preferred_element_type=F32
    )
    for n in range(4):
        r = rt_s[n * 256 : (n + 1) * 256, :].T
        for half in range(2):
            c = n * 4 + half * 2
            for zp in range(3):
                a = r[zp * 80 : zp * 80 + 40, half * 128 : half * 128 + 128]
                b = r[zp * 80 + 40 : zp * 80 + 80, half * 128 : half * 128 + 128]
                f_s[zp, pl.ds(c, 40, stride=16), :] = jnp.where(low, a, pltpu.roll(b, 64, 1))
                f_s[zp, pl.ds(c + 1, 40, stride=16), :] = jnp.where(low, pltpu.roll(a, 64, 1), b)
    for zp in range(3):
        zs_ref[zp * 576 : (zp + 1) * 576, :] = f_s[zp, 0:576, :].astype(BF16)


def combine(values, coef, row):
    total = None
    for v, val in enumerate(values):
        part = val * coef(row + 2 * v) + pltpu.roll(val, 64, 1) * coef(row + 2 * v + 1)
        total = part if total is None else total + part
    return total


def lane_in_half(rows):
    return lax.broadcasted_iota(jnp.int32, (rows, 128), 1) & 63


def pack_three(firsts, seconds, thirds):
    lane = lane_in_half(16)
    outs_a, outs_b, pieces = [], [], []
    for i in range(3):
        outs_a.append(jnp.where(lane < TERMS, firsts[i], pltpu.roll(thirds[i], 49, 1)).astype(BF16))
        outs_b.append(jnp.where(lane < TERMS, seconds[i], pltpu.roll(thirds[i], 34, 1)).astype(BF16))
        pieces.append(pltpu.roll(thirds[i], (98, 117, 8)[i], 1))
    rest = jnp.where(lane < 19, pieces[0], jnp.where(lane < 38, pieces[1], pieces[2]))
    return outs_a, outs_b, rest.astype(BF16)


def unpack_third(first, second, rest, i):
    lane = lane_in_half(16)
    tail = pltpu.roll(rest, (30, 11, 120)[i], 1)
    return jnp.where(
        lane < 15, pltpu.roll(first, 79, 1), jnp.where(lane < 30, pltpu.roll(second, 94, 1), tail)
    )


def pack_pairs(ref, base, blocks):
    low = low_lanes(16)
    for i in range(5):
        other = pltpu.roll(blocks[2 * i + 1], 64, 1) if 2 * i + 1 < 9 else blocks[2 * i]
        ref[base + i * 16 : base + (i + 1) * 16, :] = jnp.where(low, blocks[2 * i], other).astype(BF16)


def unpack_pair(ref, base, b):
    val = ref[base + (b // 2) * 16 : base + (b // 2) * 16 + 16, :].astype(F32)
    return pltpu.roll(val, 64, 1) if b % 2 else val


def parents_of(ref, up_ref):
    low = low_lanes(144)
    res = []
    for zp in range(3):
        split = ref[zp * 576 : (zp + 1) * 576, :].reshape(3, 2, 3, 2, 16, 128)
        lhs = jnp.concatenate(
            [split[:, p, :, q].reshape(144, 128) for p in range(2) for q in range(2)], axis=1
        )
        res.append(lax.dot_general(lhs, up_ref[...], NT, preferred_element_type=F32))
    return jnp.where(low, res[0], res[1]).astype(BF16), jnp.where(low, res[2], 0.0).astype(BF16)


def half_kernel(own_ref, coef_ref, up_ref, part_ref, pown_ref):
    core = lax.axis_index("gz")

    def coef(row):
        return coef_ref[core, row : row + 1, :]

    for b in range(36):
        values = [own_ref[zp * 576 + b * 16 : zp * 576 + b * 16 + 16, :].astype(F32) for zp in range(3)]
        for s in range(SLOTS):
            part_ref[s, b * 16 : b * 16 + 16, :] = combine(values, coef, s * 12)
    pown_ref[0], pown_ref[1] = parents_of(own_ref, up_ref)


def forward_kernel(part_ref, pown_ref, other_ref, coef_ref, up_ref, fa_ref, fb_ref, fo_ref, po_ref, pp_s):
    core = lax.axis_index("gz")
    odd = lax.rem(lax.axis_index("gx"), 2)

    def coef(row):
        return coef_ref[core, row : row + 1, :]

    for face, base in ((fa_ref, 3 - 3 * odd), (fb_ref, 3 * odd)):
        for xx in range(3):
            for par in range(2):
                done = [[], [], []]
                for spot in range(3):
                    at = pl.multiple_of(base * 96 + (xx * 6 + 2 * spot + par) * 16, 16)
                    values = [other_ref[pl.ds(at + zp * 576, 16), :].astype(F32) for zp in range(3)]
                    for s in range(SLOTS):
                        val = part_ref[s, pl.ds(at, 16), :] + combine(values, coef, s * 12 + 6)
                        done[s].append(val)
                        fo_ref[s, base + xx, par, spot * 16 : spot * 16 + 16, :] = val.astype(BF16)
                outs_a, outs_b, rest = pack_three(*done)
                block = xx * 2 + par
                for spot in range(3):
                    at = (block * 3 + spot) * 16
                    face[at : at + 16, :] = outs_a[spot]
                    face[288 + at : 304 + at, :] = outs_b[spot]
                face[576 + block * 16 : 592 + block * 16, :] = rest
    pp_s[0:2] = pown_ref[...]
    pp_s[2], pp_s[3] = parents_of(other_ref, up_ref)
    second = []
    for x in range(3):
        for pos in range(3):
            y = (0, 2, 1)[pos]
            at = (x * 3 + y) * 16
            values = [pp_s[v, at : at + 16, :].astype(F32) for v in range(4)]
            first = combine(values, coef, 72).astype(BF16)
            row = (x * 3 + pos) * 16
            po_ref[0, x, pos * 16 : pos * 16 + 16, :] = first
            fa_ref[672 + row : 688 + row, :] = first
            fb_ref[672 + row : 688 + row, :] = first
            val = combine(values, coef, 80)
            po_ref[1, x, pos * 16 : pos * 16 + 16, :] = val.astype(BF16)
            second.append(val)
    pack_pairs(fa_ref, 816, second)
    pack_pairs(fb_ref, 816, second)


def table_kernel(off_ref, zt_ref, far_ref, wl_ref, wp_ref, t3_s, w_s, a_s):
    core = lax.axis_index("gz")
    base = core * 80

    def spread(j, carry):
        for k in range(TERMS):
            at = pl.multiple_of(j * 104, 8) + 2 * k
            t3_s[pl.ds(at, 2), :] = far_ref[j, k].astype(F32)
        return carry

    lax.fori_loop(0, TERMS, spread, 0)
    t3_s[TERMS * 104 : 64 * 104, :] = jnp.zeros((15 * 104, 128), F32)
    for level, slots, start, out_ref in ((0, SLOTS, 0, wl_ref), (1, PSLOTS, 42, wp_ref)):
        ox = off_ref[level : level + 1, :]
        oy = off_ref[2 + level : 3 + level, :]
        oz = off_ref[4 + level : 5 + level, :]
        code = (ox + 3) * 7 + (oy + 3)
        chosen = lax.broadcasted_iota(jnp.int32, (56, 128), 0) == code
        for q in range(2 * slots):
            row = jnp.zeros((1, 128), F32)
            for d in range(7):
                row = jnp.where(oz == d - 3, zt_ref[base + start + q * 7 + d], row)
            full = jnp.where(chosen, row, 0.0)
            hi = full.astype(BF16).astype(F32)
            a_s[q * 56 : (q + 1) * 56, 0:128] = hi.astype(BF16)
            a_s[q * 56 : (q + 1) * 56, 128:256] = (full - hi).astype(BF16)
        count = slots * 56
        low = low_lanes(count)
        block = lax.broadcasted_iota(jnp.int32, (count, 128), 0)
        sign = -1.0
        if level == 0:
            sign = jnp.where(block < 56, zt_ref[base + 70], -1.0)

        def two_terms(i, carry):
            k = 2 * i
            rhs = []
            for e in range(2):
                tk = t3_s[pl.ds(2 * (k + e) + level, 64, stride=104), :].astype(BF16)
                wide = jnp.concatenate([tk, tk], axis=1)
                rhs += [wide, wide]
            out = lax.dot_general(
                a_s[0 : 2 * count, :], jnp.concatenate(rhs, axis=0), NT, preferred_element_type=F32
            )
            for e in range(2):
                even = out[0:count, e * 128 : (e + 1) * 128]
                odd = out[count : 2 * count, e * 128 : (e + 1) * 128]
                w_s[pl.ds(k + e, count, stride=136), :] = jnp.where(low, even, odd)
                w_s[pl.ds(k + e + 64, count, stride=136), :] = jnp.where(low, sign * odd, even)
            return carry

        lax.fori_loop(0, 25, two_terms, 0, unroll=5)
        inner = lax.broadcasted_iota(jnp.int32, (128, 128), 0)
        filled = (inner & 63) < TERMS

        def one_block(b, carry):
            val = w_s[pl.ds(pl.multiple_of(b * 136, 8), 128), :]
            out_ref[b] = jnp.where(filled, val, 0.0).astype(BF16)
            return carry

        lax.fori_loop(0, count, one_block, 0, unroll=4)


def weight_tiles(weights, s, diff, steps):
    d = 2 * diff + 3
    zero = jnp.zeros((128, 128), BF16)

    def weight(xi, dy):
        if dy < -3 or dy > 3:
            return zero
        return weights[s * 56 + xi * 7 + dy + 3]

    return jnp.concatenate(
        [
            jnp.concatenate([weight(xi, d + p), weight(xi, d + p - 1)], axis=1)
            for xi in steps
            for p in range(2)
        ],
        axis=0,
    )


def field_rows(field, s, steps, first, xs, rows):
    return jnp.concatenate(
        [field[s, first + xi : first + xi + xs, p].reshape(rows, 128) for xi in steps for p in range(2)],
        axis=1,
    )


def share_out(accs, s, xs, pairs, ys, put):
    spots = (ys + 1) // 2
    for pair in range(pairs):
        for o in range(2):
            yo = 2 * pair - 3 + o
            if yo >= ys + 3:
                continue
            val = None
            for diff in range(-3, 1):
                spot = pair + diff
                if 0 <= spot < spots:
                    part = accs[diff + 3][:, spot, :, o * 128 : (o + 1) * 128]
                    val = part if val is None else val + part
            for x in range(xs):
                put(s, x, yo, val[x])


SENT = ((0, 0, 2), (-1, 0, 1), (-2, 2, 3), (-3, 1, 3))
KEPT = ((0, 2, 3), (-1, 1, 3), (-2, 0, 2), (-3, 0, 1))


def spot_rows(field, s, steps, xs, span):
    rows = xs * 16 * (span[1] - span[0])
    cut = slice(span[0] * 16, span[1] * 16)
    return jnp.concatenate(
        [field[s, xi : xi + xs, p, cut].reshape(rows, 128) for xi in steps for p in range(2)], axis=1
    )


def near_kernel(fo_ref, wl_ref, acc_ref, fl_s):
    zero = jnp.zeros((SLOTS, 3, 2, 48, 128), BF16)
    fl_s[:, 0:3] = zero
    fl_s[:, 9:12] = zero
    fl_s[:, 3:9] = fo_ref[...]
    at = 0
    for s in range(SLOTS):
        for diff, lo, hi in SENT:
            lhs = spot_rows(fl_s, s, range(7), 6, (lo, hi))
            size = 96 * (hi - lo)
            acc_ref[at : at + size, :] = jnp.dot(
                lhs, weight_tiles(wl_ref, s, diff, range(7)), preferred_element_type=F32
            )
            at += size


def inner_kernel(fo_ref, fh_ref, edge_ref, wl_ref, own_ref, fl_s):
    fl_s[:, 0:3] = fh_ref[:, 0:3]
    fl_s[:, 9:12] = fh_ref[:, 3:6]
    fl_s[:, 3:9] = fo_ref[...]
    for s in range(SLOTS):
        accs = {}
        for diff, lo, hi in KEPT:
            lhs = spot_rows(fl_s, s, range(7), 6, (lo, hi))
            acc = jnp.dot(lhs, weight_tiles(wl_ref, s, diff, range(7)), preferred_element_type=F32)
            acc = acc.reshape(6, hi - lo, 16, 256)
            for spot in range(lo, hi):
                accs[diff, spot] = acc[:, spot - lo]
        for pair in (2, 3):
            val = accs[-pair, 0] + accs[1 - pair, 1] + accs[2 - pair, 2]
            for x in range(6):
                for o in range(2):
                    at = ((s * 6 + x) * 6 + 2 * pair - 3 + o) * 16
                    own_ref[at : at + 16, :] = val[x, :, o * 128 : (o + 1) * 128]
        for x in range(6):
            at = (s * 6 + x) * 96
            edge = (s * 6 + x) * 32
            own_ref[at : at + 16, :] = edge_ref[edge : edge + 16, :]
            own_ref[at + 80 : at + 96, :] = edge_ref[edge + 16 : edge + 32, :]


def far_kernel(
    a_ref, b_ref, acc_ref, po_ref, wl_ref, wp_ref, sa_ref, sb_ref, fh_ref, edge_ref, pown_ref, fl_s, fp_s, ex_s, px_s
):
    xodd = lax.rem(lax.axis_index("gx"), 2)
    yodd = lax.rem(lax.axis_index("gy"), 2)
    fl_s[:, 3:6] = jnp.zeros((SLOTS, 3, 2, 48, 128), BF16)
    fp_s[:, :, 1, 16:32] = jnp.zeros((PSLOTS, 9, 16, 128), BF16)
    part = po_ref[...]
    fp_s[:, 3:6, 0] = part[:, :, 0:32]
    fp_s[:, 3:6, 1, 0:16] = part[:, :, 32:48]
    for ref, far_side in ((a_ref, 1 - xodd), (b_ref, xodd)):
        for x in range(3):
            for par in range(2):
                block = x * 2 + par
                rest = ref[576 + block * 16 : 592 + block * 16, :].astype(F32)
                for spot in range(3):
                    at = (block * 3 + spot) * 16
                    one = ref[at : at + 16, :]
                    two = ref[288 + at : 304 + at, :]
                    three = unpack_third(one.astype(F32), two.astype(F32), rest, spot)
                    for s, val in enumerate((one, two, three.astype(BF16))):
                        fl_s[s, far_side * 6 + x, par, spot * 16 : spot * 16 + 16, :] = val
                        fh_ref[s, far_side * 3 + x, par, spot * 16 : spot * 16 + 16, :] = val
            for pos in range(3):
                b = x * 3 + pos
                pieces = (
                    ref[672 + b * 16 : 688 + b * 16, :],
                    unpack_pair(ref, 816, b).astype(BF16),
                )
                at = (pos % 2) * 16
                for s in range(PSLOTS):
                    fp_s[s, far_side * 6 + x, pos // 2, at : at + 16] = pieces[s]

    def parent_put(s, x, yo, val):
        if 0 <= yo < 3:
            at = ((s * 3 + x) * 3 + yo) * 16
            pown_ref[at : at + 16, :] = val
        else:
            px_s[0 if yo < 0 else 1, s, x * 3 + (yo + 3 if yo < 0 else yo - 3)] = val

    row = 0
    for s in range(SLOTS):
        accs = {}
        for diff, lo, hi in SENT:
            half = 48 * (hi - lo)
            for i, steps in enumerate((range(3), range(4, 7))):
                lhs = spot_rows(fl_s, s, steps, 3, (lo, hi))
                acc = acc_ref[row : row + half, :] + jnp.dot(
                    lhs, weight_tiles(wl_ref, s, diff, steps), preferred_element_type=F32
                )
                row += half
                acc = acc.reshape(3, hi - lo, 16, 256)
                for spot in range(lo, hi):
                    for x in range(3):
                        accs[diff, spot, 3 * i + x] = acc[x, spot - lo]
        for x in range(6):
            low = accs[0, 0, x]
            low_next = accs[-1, 0, x] + accs[0, 1, x]
            high_next = accs[-3, 1, x] + accs[-2, 2, x]
            high = accs[-3, 2, x]
            ex_s[0, s, x, 0] = low[:, 0:128]
            ex_s[0, s, x, 1] = low[:, 128:256]
            ex_s[0, s, x, 2] = low_next[:, 0:128]
            ex_s[1, s, x, 0] = high_next[:, 128:256]
            ex_s[1, s, x, 1] = high[:, 0:128]
            ex_s[1, s, x, 2] = high[:, 128:256]
            edge = (s * 6 + x) * 32
            edge_ref[edge : edge + 16, :] = low_next[:, 128:256]
            edge_ref[edge + 16 : edge + 32, :] = high_next[:, 0:128]
    for s in range(PSLOTS):
        lhs = field_rows(fp_s, s, range(7), 0, 3, 96)
        accs = [
            jnp.dot(lhs, weight_tiles(wp_ref, s, diff, range(7)), preferred_element_type=F32).reshape(3, 2, 16, 256)
            for diff in range(-3, 1)
        ]
        share_out(accs, s, 3, 5, 3, parent_put)
    for side, ref in ((1 - yodd, sa_ref), (yodd, sb_ref)):
        for x in range(6):
            outs_a, outs_b, rest = pack_three(
                *[[ex_s[side, s, x, i] for i in range(3)] for s in range(SLOTS)]
            )
            for i in range(3):
                at = (x * 3 + i) * 16
                ref[at : at + 16, :] = outs_a[i]
                ref[288 + at : 304 + at, :] = outs_b[i]
            ref[576 + x * 16 : 592 + x * 16, :] = rest
        for b in range(9):
            ref[672 + b * 16 : 688 + b * 16, :] = px_s[side, 0, b].astype(BF16)
        pack_pairs(ref, 816, [px_s[side, 1, b] for b in range(9)])


def join_kernel(own_ref, pown_ref, a_ref, b_ref, full_ref, zs_ref):
    yodd = lax.rem(lax.axis_index("gy"), 2)
    for ref, upper in ((a_ref, 1 - yodd), (b_ref, yodd)):
        for x in range(6):
            rest = ref[576 + x * 16 : 592 + x * 16, :].astype(F32)
            for i in range(3):
                at = (x * 3 + i) * 16
                one = ref[at : at + 16, :].astype(F32)
                two = ref[288 + at : 304 + at, :].astype(F32)
                three = unpack_third(one, two, rest, i)
                for s, val in enumerate((one, two, three)):
                    row = pl.multiple_of(((s * 6 + x) * 6 + i) * 16 + upper * 48, 16)
                    total = own_ref[pl.ds(row, 16), :] + val
                    full_ref[pl.ds(row, 16), :] = total
                    zs_ref[pl.ds(row, 16), :] = total.astype(BF16)
    for b in range(9):
        for s in range(PSLOTS):
            row = 1728 + (s * 9 + b) * 16
            total = pown_ref[row - 1728 : row - 1712, :]
            for ref in (a_ref, b_ref):
                if s == 0:
                    total = total + ref[672 + b * 16 : 688 + b * 16, :].astype(F32)
                else:
                    total = total + unpack_pair(ref, 816, b)
            full_ref[row : row + 16, :] = total
            zs_ref[row : row + 16, :] = total.astype(BF16)


def back_kernel(own_ref, coef_ref, part_ref, ppart_ref):
    core = lax.axis_index("gz")

    def coef(row):
        return coef_ref[core, row : row + 1, :]

    for i in range(9):
        at = 1728 + i * 16
        values = [own_ref[at + s * 144 : at + s * 144 + 16, :] for s in range(PSLOTS)]
        for p in range(2):
            ppart_ref[p, i * 16 : (i + 1) * 16, :] = combine(values, coef, 88 + p * 8)
    for b in range(36):
        values = [own_ref[s * 576 + b * 16 : s * 576 + b * 16 + 16, :] for s in range(SLOTS)]
        for zp in range(3):
            part_ref[zp, b * 16 : b * 16 + 16, :] = combine(values, coef, 36 + zp * 12)


def atoms_kernel(part_ref, ppart_ref, other_ref, coef_ref, one_ref, h_ref, down_ref, out_ref, pf_s, lift_s, l_s, l2_s, l3_s):
    core = lax.axis_index("gz")

    def coef(row):
        return coef_ref[core, row : row + 1, :]

    for i in range(9):
        at = 1728 + i * 16
        values = [other_ref[at + s * 144 : at + s * 144 + 16, :].astype(F32) for s in range(PSLOTS)]
        for p in range(2):
            total = ppart_ref[p, i * 16 : (i + 1) * 16, :] + combine(values, coef, 92 + p * 8)
            pf_s[p, i * 16 : (i + 1) * 16, :] = total.astype(BF16)
    for k in range(3):
        lift_s[k] = lax.dot_general(pf_s[k // 2], down_ref[k % 2], NT, preferred_element_type=F32)
    for x in range(6):
        for y in range(6):
            at = (x * 6 + y) * 16
            values = [other_ref[s * 576 + at : s * 576 + at + 16, :].astype(F32) for s in range(SLOTS)]
            par = ((x // 2) * 3 + y // 2) * 16
            lane = ((x % 2) * 2 + y % 2) * 128
            for zp in range(3):
                l_s[zp, at : at + 16, :] = (
                    part_ref[zp, at : at + 16, :]
                    + combine(values, coef, 42 + zp * 12)
                    + lift_s[zp, par : par + 16, lane : lane + 128]
                )
    low = low_lanes(40)
    for zp in range(3):
        l_s[zp, 576:640, :] = jnp.zeros((64, 128), F32)
        for cp in range(8):
            a = l_s[zp, pl.ds(2 * cp, 40, stride=16), :]
            b = l_s[zp, pl.ds(2 * cp + 1, 40, stride=16), :]
            first = jnp.where(low, a, pltpu.roll(b, 64, 1))
            second = jnp.where(low, pltpu.roll(a, 64, 1), b)
            for z, val in ((2 * zp, first), (2 * zp + 1, second)):
                hi = val.astype(BF16).astype(F32)
                l2_s[z * 40 : (z + 1) * 40, cp * 128 : (cp + 1) * 128] = hi
                l3_s[z * 40 : (z + 1) * 40, cp * 128 : (cp + 1) * 128] = val - hi
    high_rows, low_rows = [
        ref[...].T.reshape(CH, 64, 240)[:, 0:56].reshape(CH * 56, 240).astype(BF16) for ref in (l2_s, l3_s)
    ]
    for i in range(8):
        one = one_ref[:, i * 256 : (i + 1) * 256]
        spread = jnp.dot(high_rows, one, preferred_element_type=F32)
        spread = spread + jnp.dot(low_rows, one, preferred_element_type=F32)
        spread = spread.reshape(CH, 56, 256) * h_ref[0:56, i * 256 : (i + 1) * 256][None]
        out_ref[0, 0, 0, :, i * 256 : (i + 1) * 256] = jnp.sum(spread, axis=1)


def call(kernel, outs, scratch, limit, flops, moved, in_specs=None):
    placed = {} if in_specs is None else {"in_specs": in_specs}
    return pl.pallas_call(
        kernel,
        out_shape=outs,
        **placed,
        scratch_shapes=scratch,
        compiler_params=pltpu.CompilerParams(vmem_limit_bytes=limit * MIB),
        cost_estimate=pl.CostEstimate(flops=flops, bytes_accessed=moved, transcendentals=0),
    )


def shape(dims, dtype):
    return jax.ShapeDtypeStruct(dims, dtype)


def swaps(axis):
    count = lax.axis_size(axis)
    inner = [(i, i ^ 1) for i in range(count)]
    outer = [(i, (i + (1 if i % 2 else -1)) % count) for i in range(count)]
    return inner, outer


def far_weights(off, table, far):
    vmem = pl.BlockSpec(memory_space=pltpu.VMEM)
    return call(
        table_kernel,
        (shape((SLOTS * 56, 128, 128), BF16), shape((PSLOTS * 56, 128, 128), BF16)),
        [
            pltpu.VMEM((64 * 104, 128), F32),
            pltpu.VMEM((SLOTS * 56 * 136, 128), F32),
            pltpu.VMEM((SLOTS * 112, 256), BF16),
        ],
        24,
        2 * 49 * 5 * 112 * 256 * 256,
        10 * MIB,
        [vmem, pl.BlockSpec(memory_space=pltpu.SMEM), vmem],
    )(off, table, far)


def per_device(charges, positions, atom_cells, offsets, far_tables, upward_tables, downward_tables):
    up = jnp.pad(upward_tables.transpose(1, 0, 2), ((0, 15), (0, 0), (0, 15))).reshape(64, 512)
    up = jnp.concatenate([up, up], axis=0)
    down = jnp.pad(downward_tables, ((0, 0), (0, 15), (0, 15))).reshape(512, 64)
    blank = jnp.zeros_like(down)
    down = jnp.stack(
        [jnp.concatenate([down, blank], axis=1), jnp.concatenate([blank, down], axis=1)], axis=0
    )
    off = offsets.transpose(2, 0, 1).reshape(6, NOFF)
    far = far_tables.transpose(1, 2, 0, 3)
    coefs = jnp.asarray(COEFS)
    ztable = jnp.asarray(ZTABLE)
    cells = atom_cells.reshape(16, 128)
    swap = [(0, 1), (1, 0)]

    positions = pltpu.with_memory_space_constraint(positions.reshape(48, 128), pltpu.HBM)
    cells = pltpu.with_memory_space_constraint(cells, pltpu.HBM)
    leaf_z = call(
        poles_kernel,
        shape((1728, 128), BF16),
        [
            pltpu.VMEM((64, 2048), F32),
            pltpu.VMEM((240, 2048), BF16),
            pltpu.VMEM((16, 2048), BF16),
            pltpu.VMEM((48, 128), F32),
            pltpu.VMEM((16, 128), jnp.int32),
            pltpu.VMEM((1024, 128), F32),
            pltpu.VMEM((16, 2048), F32),
            pltpu.VMEM((1024, 2048), BF16),
            pltpu.VMEM((1024, 2048), BF16),
            pltpu.VMEM((1024, 240), F32),
            pltpu.VMEM((3, 640, 128), F32),
            pltpu.SemaphoreType.DMA((3,)),
        ],
        20,
        2 * 2 * 256 * 2048 * 1024,
        2 * MIB,
        [pl.BlockSpec(memory_space=pltpu.HBM)] * 3,
    )(pltpu.with_memory_space_constraint(charges, pltpu.HBM), positions, cells)
    leaf_other = lax.ppermute(leaf_z, "gz", swap)
    part, pown = call(
        half_kernel,
        (shape((SLOTS, 576, 128), F32), shape((2, 144, 128), BF16)),
        [],
        8,
        1 << 27,
        2 * MIB,
    )(leaf_z, coefs, up)
    face = shape((896, 128), BF16)
    fa, fb, fo, po = call(
        forward_kernel,
        (face, face, shape((SLOTS, 6, 2, 48, 128), BF16), shape((PSLOTS, 3, 48, 128), BF16)),
        [pltpu.VMEM((4, 144, 128), BF16)],
        8,
        1 << 28,
        2 * MIB,
    )(part, pown, leaf_other, coefs, up)
    inner, outer = swaps("gx")
    fa = lax.ppermute(fa, "gx", inner)
    fb = lax.ppermute(fb, "gx", outer)
    fo, off = lax.optimization_barrier((fo, off))
    wl, wp = far_weights(off, ztable, far)
    near = call(
        near_kernel,
        shape((SLOTS * 576, 256), F32),
        [pltpu.VMEM((SLOTS, 12, 2, 48, 128), BF16)],
        16,
        2 * 144 * 1792 * 256 * 12,
        8 * MIB,
    )(fo, wl)
    sa, sb, fh, edge, pown = call(
        far_kernel,
        (
            face,
            face,
            shape((SLOTS, 6, 2, 48, 128), BF16),
            shape((SLOTS * 192, 128), F32),
            shape((288, 128), F32),
        ),
        [
            pltpu.VMEM((SLOTS, 9, 2, 48, 128), BF16),
            pltpu.VMEM((PSLOTS, 9, 2, 32, 128), BF16),
            pltpu.VMEM((2, SLOTS, 6, 3, 16, 128), F32),
            pltpu.VMEM((2, PSLOTS, 9, 16, 128), F32),
        ],
        16,
        2 * 288 * 1792 * 256 * 8,
        14 * MIB,
    )(fa, fb, near, po, wl, wp)
    inner, outer = swaps("gy")
    sa = lax.ppermute(sa, "gy", inner)
    sb = lax.ppermute(sb, "gy", outer)
    edge, positions, cells = lax.optimization_barrier((edge, positions, cells))
    own = call(
        inner_kernel,
        shape((1728, 128), F32),
        [pltpu.VMEM((SLOTS, 12, 2, 48, 128), BF16)],
        16,
        2 * 144 * 1792 * 256 * 12,
        8 * MIB,
    )(fo, fh, edge, wl)
    harm, one = call(
        atom_terms_kernel,
        (shape((64, 2048), F32), shape((240, 2048), BF16)),
        [pltpu.VMEM((1024, 128), F32)],
        8,
        1 << 24,
        2 * MIB,
    )(positions, cells)
    own, harm, one = lax.optimization_barrier((own, harm, one))
    full, zsend = call(
        join_kernel, (shape((2016, 128), F32), shape((2016, 128), BF16)), [], 8, 1 << 20, 3 * MIB
    )(own, pown, sa, sb)
    zrecv = lax.ppermute(zsend, "gz", swap)
    part, ppart = call(
        back_kernel,
        (shape((SLOTS, 576, 128), F32), shape((2, 144, 128), F32)),
        [],
        8,
        1 << 24,
        2 * MIB,
    )(full, coefs)
    potential = call(
        atoms_kernel,
        shape((1, 1, 1, CH, 2048), F32),
        [
            pltpu.VMEM((2, 144, 128), BF16),
            pltpu.VMEM((3, 144, 512), F32),
            pltpu.VMEM((3, 640, 128), F32),
            pltpu.VMEM((240, 1024), F32),
            pltpu.VMEM((240, 1024), F32),
        ],
        16,
        2 * 2 * 256 * 2048 * 1024,
        2 * MIB,
    )(part, ppart, zrecv, coefs, one, harm, down)
    return potential


def solution(mesh):
    placed = (
        P("gx", "gy", "gz", None, None),
        P("gx", "gy", "gz", None, None),
        P("gx", "gy", "gz", None),
        P(),
        P(),
        P(),
        P(),
    )
    return jax.shard_map(
        per_device,
        mesh=mesh,
        in_specs=placed,
        out_specs=P("gx", "gy", "gz", None, None),
        check_vma=False,
    )
```

```python
import math

import numpy as np
import jax
import jax.numpy as jnp
from jax import lax
from jax.experimental import pallas as pl
from jax.experimental.pallas import tpu as pltpu
from jax.sharding import PartitionSpec as P

CH = 16
ORDER = 6
TERMS = 49
NOFF = 128
SLOTS = 3
PSLOTS = 2
F32 = jnp.float32
BF16 = jnp.bfloat16
NT = (((1,), (1,)), ((), ()))
TN = (((0,), (0,)), ((), ()))
radial_scale = 1.6
MIB = 1 << 20


def spectral_constants():
    leaf_freq = [[None, 2, 4], [1, 3, 5]]
    pair_freq = [[2, 0], [1, 3]]
    turn = 2 * math.pi / 12
    pturn = 2 * math.pi / 6

    def fwd(core, s, ri, z):
        f = leaf_freq[core][s]
        if f is None:
            return float(z % 2 == ri)
        return math.cos(turn * f * z) if ri == 0 else -math.sin(turn * f * z)

    def inv(core, s, ri, z):
        f = leaf_freq[core][s]
        if f is None:
            return float(z % 2 == ri) / 6
        return (math.cos(turn * f * z) if ri == 0 else -math.sin(turn * f * z)) / 6

    def pfwd(core, s, ri, z):
        f = pair_freq[core][s]
        if s == 1:
            return math.cos(pturn * f * z) if ri == 0 else 0.0
        return math.cos(pturn * f * z) if ri == 0 else -math.sin(pturn * f * z)

    def pinv(core, s, ri, z):
        return pfwd(core, s, ri, z) / (6 if s == 1 else 3)

    halves = np.zeros((2, 104, 128))
    for core in range(2):
        row = 0

        def put(a, b):
            nonlocal row
            halves[core, row, :64] = a
            halves[core, row, 64:] = b
            row += 1

        for s in range(SLOTS):
            for v in range(6):
                z = (core if v < 3 else 1 - core) * 6 + 2 * (v % 3)
                put(fwd(core, s, 0, z), fwd(core, s, 1, z + 1))
                put(fwd(core, s, 0, z + 1), fwd(core, s, 1, z))
        for p in range(3):
            z = core * 6 + 2 * p
            for u in range(6):
                own = core if u < 3 else 1 - core
                s = u % 3
                put(inv(own, s, 0, z), inv(own, s, 1, z + 1))
                put(inv(own, s, 1, z), inv(own, s, 0, z + 1))
        for s in range(PSLOTS):
            for v in range(4):
                z = (core if v < 2 else 1 - core) * 3 + 2 * (v % 2)
                on = float(v % 2 == 0)
                put(pfwd(core, s, 0, z), on * pfwd(core, s, 1, z + 1))
                put(on * pfwd(core, s, 0, z + 1), pfwd(core, s, 1, z))
        for p in range(2):
            z = core * 3 + 2 * p
            on = float(p == 0)
            for u in range(4):
                own = core if u < 2 else 1 - core
                s = u % 2
                put(pinv(own, s, 0, z), on * pinv(own, s, 1, z + 1))
                put(pinv(own, s, 1, z), on * pinv(own, s, 0, z + 1))
        assert row == 104
    table = np.zeros((2, 80))
    for core in range(2):
        for pq in range(2):
            for s in range(SLOTS):
                f = leaf_freq[core][s]
                for d in range(7):
                    dz = d - 3
                    if f is None:
                        val = float(dz % 2 == pq)
                    else:
                        val = math.sin(turn * f * dz) if pq else math.cos(turn * f * dz)
                    table[core, (pq * SLOTS + s) * 7 + d] = val
            for s in range(PSLOTS):
                f = pair_freq[core][s]
                for d in range(7):
                    dz = d - 3
                    if s == 1:
                        val = 0.0 if pq else math.cos(pturn * f * dz)
                    else:
                        val = math.sin(pturn * f * dz) if pq else math.cos(pturn * f * dz)
                    table[core, 42 + (pq * PSLOTS + s) * 7 + d] = val
        table[core, 70] = 1.0 if core == 0 else -1.0
    return halves.astype(np.float32), table.reshape(-1).astype(np.float32)


COEFS, ZTABLE = spectral_constants()


def harmonic_terms(x, y, z):
    rsq = x * x + y * y + z * z
    cosines = {(0, 0): jnp.ones_like(x)}
    sines = {}
    for deg in range(1, ORDER + 1):
        for m in range(deg):
            inv = 1.0 / float((deg + m) * (deg - m))
            for part in (cosines, sines):
                if part is sines and m == 0:
                    continue
                val = ((2 * deg - 1) * inv) * (z * part[deg - 1, m])
                if m <= deg - 2:
                    val = val - inv * (rsq * part[deg - 2, m])
                part[deg, m] = val
        scale = -1.0 / (2.0 * deg)
        pc = cosines[deg - 1, deg - 1]
        if deg == 1:
            cosines[1, 1] = scale * x
            sines[1, 1] = scale * y
        else:
            ps = sines[deg - 1, deg - 1]
            cosines[deg, deg] = scale * (x * pc - y * ps)
            sines[deg, deg] = scale * (x * ps + y * pc)
    out = []
    for deg in range(ORDER + 1):
        out.append(cosines[deg, 0] * float(math.factorial(deg)))
        for m in range(1, deg + 1):
            factor = math.sqrt(math.factorial(deg + m) * math.factorial(deg - m))
            out.append(cosines[deg, m] * factor)
            out.append(sines[deg, m] * factor)
    return out


def low_lanes(rows):
    return lax.broadcasted_iota(jnp.int32, (rows, 128), 1) < 64


def cell_number_rows():
    row = lax.broadcasted_iota(jnp.int32, (240, 128), 0)
    z = jnp.zeros_like(row)
    for i in range(1, 6):
        z = z + (row >= 40 * i).astype(jnp.int32)
    xy = row - 40 * z
    return jnp.where(xy < 36, xy * 6 + z, -1)


def start_copies(pairs, sems):
    copies = [pltpu.make_async_copy(src, dst, sems.at[i]) for i, (src, dst) in enumerate(pairs)]
    for copy in copies:
        copy.start()
    return copies


def fill_harmonics(pos_s, h3_s, h_ref):
    terms = harmonic_terms(
        radial_scale * pos_s[0:16, :], radial_scale * pos_s[16:32, :], radial_scale * pos_s[32:48, :]
    )
    for k in range(TERMS):
        h3_s[k * 16 : (k + 1) * 16, :] = terms[k]
    h3_s[TERMS * 16 : 1024, :] = jnp.zeros((1024 - TERMS * 16, 128), F32)
    for i in range(16):
        h_ref[:, i * 128 : (i + 1) * 128] = h3_s[pl.ds(i, 64, stride=16), :]


def fill_onehot(cell_s, one_ref):
    number = cell_number_rows()
    for i in range(16):
        one_ref[:, i * 128 : (i + 1) * 128] = jnp.where(number == cell_s[i : i + 1, :], 1.0, 0.0).astype(BF16)


def atom_terms_kernel(pos_ref, cell_ref, h_ref, one_ref, h3_s):
    fill_harmonics(pos_ref, h3_s, h_ref)
    fill_onehot(cell_ref, one_ref)


def poles_kernel(ch_hbm, pos_hbm, cell_hbm, zs_ref, h_s, one_s, ch_s, pos_s, cell_s, h3_s, chf_s, whi_s, wlo_s, f_s, sems):
    copies = start_copies(((pos_hbm, pos_s), (cell_hbm, cell_s), (ch_hbm.at[0, 0, 0], ch_s)), sems)
    copies[0].wait()
    fill_harmonics(pos_s, h3_s, h_s)
    copies[1].wait()
    fill_onehot(cell_s, one_s)
    copies[2].wait()
    chf_s[...] = ch_s[...].astype(F32)
    low = low_lanes(40)
    for n in range(4):
        for c in range(4 * n, 4 * n + 4):
            for i in range(4):
                sl = slice(i * 512, (i + 1) * 512)
                w = h_s[:, sl] * chf_s[c : c + 1, sl]
                hi = w.astype(BF16)
                whi_s[c * 64 : (c + 1) * 64, sl] = hi
                wlo_s[c * 64 : (c + 1) * 64, sl] = (w - hi.astype(F32)).astype(BF16)
        rows = slice(n * 256, (n + 1) * 256)
        r = lax.dot_general(one_s[...], whi_s[rows, :], NT, preferred_element_type=F32)
        r = r + lax.dot_general(one_s[...], wlo_s[rows, :], NT, preferred_element_type=F32)
        for half in range(2):
            c = n * 4 + half * 2
            for zp in range(3):
                a = r[zp * 80 : zp * 80 + 40, half * 128 : half * 128 + 128]
                b = r[zp * 80 + 40 : zp * 80 + 80, half * 128 : half * 128 + 128]
                f_s[zp, pl.ds(c, 40, stride=16), :] = jnp.where(low, a, pltpu.roll(b, 64, 1))
                f_s[zp, pl.ds(c + 1, 40, stride=16), :] = jnp.where(low, pltpu.roll(a, 64, 1), b)
    for zp in range(3):
        zs_ref[zp * 576 : (zp + 1) * 576, :] = f_s[zp, 0:576, :].astype(BF16)


def combine(values, coef, row):
    total = None
    for v, val in enumerate(values):
        part = val * coef(row + 2 * v) + pltpu.roll(val, 64, 1) * coef(row + 2 * v + 1)
        total = part if total is None else total + part
    return total


def lane_in_half(rows):
    return lax.broadcasted_iota(jnp.int32, (rows, 128), 1) & 63


def pack_three(firsts, seconds, thirds):
    lane = lane_in_half(16)
    outs_a, outs_b, pieces = [], [], []
    for i in range(3):
        outs_a.append(jnp.where(lane < TERMS, firsts[i], pltpu.roll(thirds[i], 49, 1)).astype(BF16))
        outs_b.append(jnp.where(lane < TERMS, seconds[i], pltpu.roll(thirds[i], 34, 1)).astype(BF16))
        pieces.append(pltpu.roll(thirds[i], (98, 117, 8)[i], 1))
    rest = jnp.where(lane < 19, pieces[0], jnp.where(lane < 38, pieces[1], pieces[2]))
    return outs_a, outs_b, rest.astype(BF16)


def unpack_third(first, second, rest, i):
    lane = lane_in_half(16)
    tail = pltpu.roll(rest, (30, 11, 120)[i], 1)
    return jnp.where(
        lane < 15, pltpu.roll(first, 79, 1), jnp.where(lane < 30, pltpu.roll(second, 94, 1), tail)
    )


def rest_shift(b):
    piece = b % 6
    return (64 * (piece // 3) + 19 * (piece % 3) - 30) % 128


def pack_parents(refs, firsts, seconds):
    lane = lax.broadcasted_iota(jnp.int32, (16, 128), 1)
    inner = lane & 63
    for b in range(9):
        spare = jnp.where(lane < 64, pltpu.roll(seconds[b], 49, 1), pltpu.roll(seconds[b], 98, 1))
        val = jnp.where(inner < TERMS, firsts[b], spare).astype(BF16)
        for ref in refs:
            ref[672 + b * 16 : 688 + b * 16, :] = val
    for i in range(2):
        pieces = [pltpu.roll(seconds[b], rest_shift(b), 1) for b in range(6 * i, min(6 * i + 6, 9))]
        halves = [
            jnp.where(inner < 19, part[0], jnp.where(inner < 38, part[1], part[2]))
            for part in (pieces[0:3], pieces[-3:])
        ]
        val = jnp.where(lane < 64, halves[0], halves[1]).astype(BF16)
        for ref in refs:
            ref[816 + i * 16 : 832 + i * 16, :] = val


def side_by_side(vals):
    low = low_lanes(16)
    first = jnp.where(low, vals[0], pltpu.roll(vals[2], 64, 1))
    return jnp.concatenate([first, jnp.where(low, vals[1], 0.0)], axis=0).astype(BF16)


def unpack_second(ref, b):
    lane = lax.broadcasted_iota(jnp.int32, (16, 128), 1)
    first = ref[672 + b * 16 : 688 + b * 16, :].astype(F32)
    rest = ref[816 + b // 6 * 16 : 832 + b // 6 * 16, :].astype(F32)
    tail = pltpu.roll(rest, (128 - rest_shift(b)) % 128, 1)
    return jnp.where(lane < 15, pltpu.roll(first, 79, 1), jnp.where(lane < 30, pltpu.roll(first, 30, 1), tail))


def parents_of(ref, up_ref):
    low = low_lanes(144)
    res = []
    for zp in range(3):
        split = ref[zp * 576 : (zp + 1) * 576, :].reshape(3, 2, 3, 2, 16, 128)
        lhs = jnp.concatenate(
            [split[:, p, :, q].reshape(144, 128) for p in range(2) for q in range(2)], axis=1
        )
        res.append(lax.dot_general(lhs, up_ref[...], NT, preferred_element_type=F32))
    return jnp.where(low, res[0], res[1]).astype(BF16), jnp.where(low, res[2], 0.0).astype(BF16)


def half_kernel(own_ref, coef_ref, up_ref, part_ref, pown_ref):
    core = lax.axis_index("gz")

    def coef(row):
        return coef_ref[core, row : row + 1, :]

    for b in range(36):
        values = [own_ref[zp * 576 + b * 16 : zp * 576 + b * 16 + 16, :].astype(F32) for zp in range(3)]
        for s in range(SLOTS):
            part_ref[s, b * 16 : b * 16 + 16, :] = combine(values, coef, s * 12)
    pown_ref[0], pown_ref[1] = parents_of(own_ref, up_ref)


def forward_kernel(part_ref, pown_ref, other_ref, coef_ref, up_ref, fb_ref, fa_ref, fo_ref, po_ref, pq_ref, pp_s):
    core = lax.axis_index("gz")
    odd = lax.rem(lax.axis_index("gx"), 2)

    def coef(row):
        return coef_ref[core, row : row + 1, :]

    for face, base in ((fa_ref, 3 - 3 * odd), (fb_ref, 3 * odd)):
        for xx in range(3):
            for par in range(2):
                done = [[], [], []]
                for spot in range(3):
                    at = pl.multiple_of(base * 96 + (xx * 6 + 2 * spot + par) * 16, 16)
                    values = [other_ref[pl.ds(at + zp * 576, 16), :].astype(F32) for zp in range(3)]
                    for s in range(SLOTS):
                        val = part_ref[s, pl.ds(at, 16), :] + combine(values, coef, s * 12 + 6)
                        done[s].append(val)
                        fo_ref[s, base + xx, par, spot * 16 : spot * 16 + 16, :] = val.astype(BF16)
                outs_a, outs_b, rest = pack_three(*done)
                block = xx * 2 + par
                for spot in range(3):
                    at = (block * 3 + spot) * 16
                    face[at : at + 16, :] = outs_a[spot]
                    face[288 + at : 304 + at, :] = outs_b[spot]
                face[576 + block * 16 : 592 + block * 16, :] = rest
    pp_s[0:2] = pown_ref[...]
    pp_s[2], pp_s[3] = parents_of(other_ref, up_ref)
    firsts, seconds = [], []
    for x in range(3):
        for pos in range(3):
            at = (x * 3 + (0, 2, 1)[pos]) * 16
            values = [pp_s[v, at : at + 16, :].astype(F32) for v in range(4)]
            firsts.append(combine(values, coef, 72))
            seconds.append(combine(values, coef, 80))
            po_ref[x, pos * 16 : pos * 16 + 16, :] = firsts[-1].astype(BF16)
        pq_ref[x] = side_by_side(seconds[3 * x : 3 * x + 3])
    pack_parents((fa_ref, fb_ref), firsts, seconds)


def table_kernel(off_ref, zt_ref, far_ref, wl_ref, wp_ref, wq_ref, t3_s, w_s, a_s):
    core = lax.axis_index("gz")
    base = core * 80

    def spread(j, carry):
        for k in range(TERMS):
            at = pl.multiple_of(j * 104, 8) + 2 * k
            t3_s[pl.ds(at, 2), :] = far_ref[j, k].astype(F32)
        return carry

    lax.fori_loop(0, TERMS, spread, 0)
    t3_s[TERMS * 104 : 64 * 104, :] = jnp.zeros((15 * 104, 128), F32)
    for level, slots, start, out_ref in ((0, SLOTS, 0, wl_ref), (1, PSLOTS, 42, wp_ref)):
        ox = off_ref[level : level + 1, :]
        oy = off_ref[2 + level : 3 + level, :]
        oz = off_ref[4 + level : 5 + level, :]
        code = (ox + 3) * 7 + (oy + 3)
        chosen = lax.broadcasted_iota(jnp.int32, (56, 128), 0) == code
        for q in range(2 * slots):
            row = jnp.zeros((1, 128), F32)
            for d in range(7):
                row = jnp.where(oz == d - 3, zt_ref[base + start + q * 7 + d], row)
            full = jnp.where(chosen, row, 0.0)
            hi = full.astype(BF16).astype(F32)
            a_s[q * 56 : (q + 1) * 56, 0:128] = hi.astype(BF16)
            a_s[q * 56 : (q + 1) * 56, 128:256] = (full - hi).astype(BF16)
        count = slots * 56
        low = low_lanes(count)
        block = lax.broadcasted_iota(jnp.int32, (count, 128), 0)
        sign = -1.0
        both = low
        if level == 0:
            sign = jnp.where(block < 56, zt_ref[base + 70], -1.0)
        else:
            both = low | (block >= 56)
        turned = 168 if level == 0 else 56

        def two_terms(i, carry):
            k = 2 * i
            rhs = []
            for e in range(2):
                tk = t3_s[pl.ds(2 * (k + e) + level, 64, stride=104), :].astype(BF16)
                wide = jnp.concatenate([tk, tk], axis=1)
                rhs += [wide, wide]
            out = lax.dot_general(
                a_s[0 : 2 * count, :], jnp.concatenate(rhs, axis=0), NT, preferred_element_type=F32
            )
            for e in range(2):
                even = out[0:count, e * 128 : (e + 1) * 128]
                odd = out[count : 2 * count, e * 128 : (e + 1) * 128]
                w_s[pl.ds(k + e, count, stride=136), :] = jnp.where(both, even, odd)
                w_s[pl.ds(k + e + 64, turned, stride=136), :] = jnp.where(low, sign * odd, even)[0:turned]
            return carry

        lax.fori_loop(0, 25, two_terms, 0, unroll=5)
        inner = lax.broadcasted_iota(jnp.int32, (128, 128), 0)
        filled = (inner & 63) < TERMS

        def one_block(b, carry):
            val = w_s[pl.ds(pl.multiple_of(b * 136, 8), 128), :]
            out_ref[b] = jnp.where(filled, val, 0.0).astype(BF16)
            return carry

        lax.fori_loop(0, turned, one_block, 0, unroll=4)
    half = low_lanes(64)
    kept = lax.broadcasted_iota(jnp.int32, (64, 128), 0) < TERMS

    def one_step(xi, carry):
        def block_of(dy):
            if dy < -3 or dy > 3:
                return jnp.zeros((64, 128), F32)
            return w_s[pl.ds(pl.multiple_of((56 + xi * 7 + dy + 3) * 136, 8), 64), :]

        for i in range(4):
            d = 2 * i - 3
            for p in range(2):
                val = jnp.where(half, block_of(d + p), block_of(d + p - 1))
                wq_ref[xi, p * 64 : p * 64 + 64, i * 128 : (i + 1) * 128] = jnp.where(kept, val, 0.0).astype(BF16)
        return carry

    lax.fori_loop(0, 7, one_step, 0)


def weight_tiles(weights, s, diff, steps):
    d = 2 * diff + 3
    zero = jnp.zeros((128, 128), BF16)

    def weight(xi, dy):
        if dy < -3 or dy > 3:
            return zero
        return weights[s * 56 + xi * 7 + dy + 3]

    return jnp.concatenate(
        [
            jnp.concatenate([weight(xi, d + p), weight(xi, d + p - 1)], axis=1)
            for xi in steps
            for p in range(2)
        ],
        axis=0,
    )


def field_rows(field, s, steps, first, xs, rows):
    return jnp.concatenate(
        [field[s, first + xi : first + xi + xs, p].reshape(rows, 128) for xi in steps for p in range(2)],
        axis=1,
    )


def share_out(accs, s, xs, pairs, ys, put):
    spots = (ys + 1) // 2
    for pair in range(pairs):
        for o in range(2):
            yo = 2 * pair - 3 + o
            if yo >= ys + 3:
                continue
            val = None
            for diff in range(-3, 1):
                spot = pair + diff
                if 0 <= spot < spots:
                    part = accs[diff + 3][:, spot, :, o * 128 : (o + 1) * 128]
                    val = part if val is None else val + part
            for x in range(xs):
                put(s, x, yo, val[x])


SENT = ((0, 0, 2), (-1, 0, 1), (-2, 2, 3), (-3, 1, 3))
KEPT = ((0, 2, 3), (-1, 1, 3), (-2, 0, 2), (-3, 0, 1))


def spot_rows(field, s, steps, xs, span):
    rows = xs * 16 * (span[1] - span[0])
    cut = slice(span[0] * 16, span[1] * 16)
    return jnp.concatenate(
        [field[s, xi : xi + xs, p, cut].reshape(rows, 128) for xi in steps for p in range(2)], axis=1
    )


def near_kernel(fo_ref, wl_ref, acc_ref, fl_s):
    zero = jnp.zeros((SLOTS, 3, 2, 48, 128), BF16)
    fl_s[:, 0:3] = zero
    fl_s[:, 9:12] = zero
    fl_s[:, 3:9] = fo_ref[...]
    at = 0
    for s in range(SLOTS):
        for diff, lo, hi in SENT:
            lhs = spot_rows(fl_s, s, range(7), 6, (lo, hi))
            size = 96 * (hi - lo)
            acc_ref[at : at + size, :] = jnp.dot(
                lhs, weight_tiles(wl_ref, s, diff, range(7)), preferred_element_type=F32
            )
            at += size


def inner_kernel(fo_ref, fh_ref, edge_ref, wl_ref, own_ref, fl_s):
    fl_s[:, 0:3] = fh_ref[:, 0:3]
    fl_s[:, 9:12] = fh_ref[:, 3:6]
    fl_s[:, 3:9] = fo_ref[...]
    for s in range(SLOTS):
        accs = {}
        for diff, lo, hi in KEPT:
            lhs = spot_rows(fl_s, s, range(7), 6, (lo, hi))
            acc = jnp.dot(lhs, weight_tiles(wl_ref, s, diff, range(7)), preferred_element_type=F32)
            acc = acc.reshape(6, hi - lo, 16, 256)
            for spot in range(lo, hi):
                accs[diff, spot] = acc[:, spot - lo]
        for pair in (2, 3):
            val = accs[-pair, 0] + accs[1 - pair, 1] + accs[2 - pair, 2]
            for x in range(6):
                for o in range(2):
                    at = ((s * 6 + x) * 6 + 2 * pair - 3 + o) * 16
                    own_ref[at : at + 16, :] = val[x, :, o * 128 : (o + 1) * 128]
        for x in range(6):
            at = (s * 6 + x) * 96
            edge = (s * 6 + x) * 32
            own_ref[at : at + 16, :] = edge_ref[edge : edge + 16, :]
            own_ref[at + 80 : at + 96, :] = edge_ref[edge + 16 : edge + 32, :]


def far_kernel(
    b_ref, a_ref, acc_ref, po_ref, pq_ref, wl_ref, wp_ref, wq_ref,
    sb_ref, sa_ref, fh_ref, edge_ref, pown_ref, fl_s, fp_s, fq_s, ex_s, px_s
):
    xodd = lax.rem(lax.axis_index("gx"), 2)
    yodd = lax.rem(lax.axis_index("gy"), 2)
    fl_s[:, 3:6] = jnp.zeros((SLOTS, 3, 2, 48, 128), BF16)
    fp_s[0, :, 1, 16:32] = jnp.zeros((9, 16, 128), BF16)
    part = po_ref[...]
    fp_s[0, 3:6, 0] = part[:, 0:32]
    fp_s[0, 3:6, 1, 0:16] = part[:, 32:48]
    fq_s[3:6] = pq_ref[...]
    for ref, far_side in ((a_ref, 1 - xodd), (b_ref, xodd)):
        for x in range(3):
            for par in range(2):
                block = x * 2 + par
                rest = ref[576 + block * 16 : 592 + block * 16, :].astype(F32)
                for spot in range(3):
                    at = (block * 3 + spot) * 16
                    one = ref[at : at + 16, :]
                    two = ref[288 + at : 304 + at, :]
                    three = unpack_third(one.astype(F32), two.astype(F32), rest, spot)
                    for s, val in enumerate((one, two, three.astype(BF16))):
                        fl_s[s, far_side * 6 + x, par, spot * 16 : spot * 16 + 16, :] = val
                        fh_ref[s, far_side * 3 + x, par, spot * 16 : spot * 16 + 16, :] = val
            for pos in range(3):
                b = x * 3 + pos
                at = (pos % 2) * 16
                fp_s[0, far_side * 6 + x, pos // 2, at : at + 16] = ref[672 + b * 16 : 688 + b * 16, :]
            fq_s[far_side * 6 + x] = side_by_side([unpack_second(ref, x * 3 + pos) for pos in range(3)])

    def parent_put(s, x, yo, val):
        if 0 <= yo < 3:
            at = ((s * 3 + x) * 3 + yo) * 16
            pown_ref[at : at + 16, :] = val
        else:
            px_s[0 if yo < 0 else 1, s, x * 3 + (yo + 3 if yo < 0 else yo - 3)] = val

    row = 0
    for s in range(SLOTS):
        accs = {}
        for diff, lo, hi in SENT:
            half = 48 * (hi - lo)
            for i, steps in enumerate((range(3), range(4, 7))):
                lhs = spot_rows(fl_s, s, steps, 3, (lo, hi))
                acc = acc_ref[row : row + half, :] + jnp.dot(
                    lhs, weight_tiles(wl_ref, s, diff, steps), preferred_element_type=F32
                )
                row += half
                acc = acc.reshape(3, hi - lo, 16, 256)
                for spot in range(lo, hi):
                    for x in range(3):
                        accs[diff, spot, 3 * i + x] = acc[x, spot - lo]
        for x in range(6):
            low = accs[0, 0, x]
            low_next = accs[-1, 0, x] + accs[0, 1, x]
            high_next = accs[-3, 1, x] + accs[-2, 2, x]
            high = accs[-3, 2, x]
            ex_s[0, s, x, 0] = low[:, 0:128]
            ex_s[0, s, x, 1] = low[:, 128:256]
            ex_s[0, s, x, 2] = low_next[:, 0:128]
            ex_s[1, s, x, 0] = high_next[:, 128:256]
            ex_s[1, s, x, 1] = high[:, 0:128]
            ex_s[1, s, x, 2] = high[:, 128:256]
            edge = (s * 6 + x) * 32
            edge_ref[edge : edge + 16, :] = low_next[:, 128:256]
            edge_ref[edge + 16 : edge + 32, :] = high_next[:, 0:128]
    lhs = field_rows(fp_s, 0, range(7), 0, 3, 96)
    accs = [
        jnp.dot(lhs, weight_tiles(wp_ref, 0, diff, range(7)), preferred_element_type=F32).reshape(3, 2, 16, 256)
        for diff in range(-3, 1)
    ]
    share_out(accs, 0, 3, 5, 3, parent_put)
    lhs = jnp.concatenate([fq_s[xi : xi + 3].reshape(96, 128) for xi in range(7)], axis=1)
    acc = jnp.dot(lhs, wq_ref[...].reshape(896, 512), preferred_element_type=F32).reshape(3, 2, 16, 512)
    for pair in range(5):
        val = None
        for diff in range(-3, 1):
            spot = pair + diff
            if 0 <= spot < 2:
                piece = acc[:, spot, :, (diff + 3) * 128 : (diff + 4) * 128]
                val = piece if val is None else val + piece
        for x in range(3):
            parent_put(1, x, 2 * pair - 3, val[x])
            if pair < 4:
                parent_put(1, x, 2 * pair - 2, pltpu.roll(val[x], 64, 1))
    for side, ref in ((1 - yodd, sa_ref), (yodd, sb_ref)):
        for x in range(6):
            outs_a, outs_b, rest = pack_three(
                *[[ex_s[side, s, x, i] for i in range(3)] for s in range(SLOTS)]
            )
            for i in range(3):
                at = (x * 3 + i) * 16
                ref[at : at + 16, :] = outs_a[i]
                ref[288 + at : 304 + at, :] = outs_b[i]
            ref[576 + x * 16 : 592 + x * 16, :] = rest
        pack_parents((ref,), *[[px_s[side, s, b] for b in range(9)] for s in range(PSLOTS)])


def join_kernel(own_ref, pown_ref, b_ref, a_ref, full_ref, zs_ref):
    yodd = lax.rem(lax.axis_index("gy"), 2)
    for ref, upper in ((a_ref, 1 - yodd), (b_ref, yodd)):
        for x in range(6):
            rest = ref[576 + x * 16 : 592 + x * 16, :].astype(F32)
            for i in range(3):
                at = (x * 3 + i) * 16
                one = ref[at : at + 16, :].astype(F32)
                two = ref[288 + at : 304 + at, :].astype(F32)
                three = unpack_third(one, two, rest, i)
                for s, val in enumerate((one, two, three)):
                    row = pl.multiple_of(((s * 6 + x) * 6 + i) * 16 + upper * 48, 16)
                    total = own_ref[pl.ds(row, 16), :] + val
                    full_ref[pl.ds(row, 16), :] = total
                    zs_ref[pl.ds(row, 16), :] = total.astype(BF16)
    for b in range(9):
        for s in range(PSLOTS):
            row = 1728 + (s * 9 + b) * 16
            total = pown_ref[row - 1728 : row - 1712, :]
            for ref in (a_ref, b_ref):
                if s == 0:
                    total = total + ref[672 + b * 16 : 688 + b * 16, :].astype(F32)
                else:
                    total = total + unpack_second(ref, b)
            full_ref[row : row + 16, :] = total
            zs_ref[row : row + 16, :] = total.astype(BF16)


def back_kernel(own_ref, coef_ref, part_ref, ppart_ref):
    core = lax.axis_index("gz")

    def coef(row):
        return coef_ref[core, row : row + 1, :]

    for i in range(9):
        at = 1728 + i * 16
        values = [own_ref[at + s * 144 : at + s * 144 + 16, :] for s in range(PSLOTS)]
        for p in range(2):
            ppart_ref[p, i * 16 : (i + 1) * 16, :] = combine(values, coef, 88 + p * 8)
    for b in range(36):
        values = [own_ref[s * 576 + b * 16 : s * 576 + b * 16 + 16, :] for s in range(SLOTS)]
        for zp in range(3):
            part_ref[zp, b * 16 : b * 16 + 16, :] = combine(values, coef, 36 + zp * 12)


def atoms_kernel(part_ref, ppart_ref, other_ref, coef_ref, one_ref, h_ref, down_ref, out_ref, pf_s, lift_s, l_s, l2_s, l3_s):
    core = lax.axis_index("gz")

    def coef(row):
        return coef_ref[core, row : row + 1, :]

    for i in range(9):
        at = 1728 + i * 16
        values = [other_ref[at + s * 144 : at + s * 144 + 16, :].astype(F32) for s in range(PSLOTS)]
        for p in range(2):
            total = ppart_ref[p, i * 16 : (i + 1) * 16, :] + combine(values, coef, 92 + p * 8)
            pf_s[p, i * 16 : (i + 1) * 16, :] = total.astype(BF16)
    for k in range(3):
        lift_s[k] = lax.dot_general(pf_s[k // 2], down_ref[k % 2], NT, preferred_element_type=F32)
    for x in range(6):
        for y in range(6):
            at = (x * 6 + y) * 16
            values = [other_ref[s * 576 + at : s * 576 + at + 16, :].astype(F32) for s in range(SLOTS)]
            par = ((x // 2) * 3 + y // 2) * 16
            lane = ((x % 2) * 2 + y % 2) * 128
            for zp in range(3):
                l_s[zp, at : at + 16, :] = (
                    part_ref[zp, at : at + 16, :]
                    + combine(values, coef, 42 + zp * 12)
                    + lift_s[zp, par : par + 16, lane : lane + 128]
                )
    low = low_lanes(40)
    for zp in range(3):
        l_s[zp, 576:640, :] = jnp.zeros((64, 128), F32)
        for cp in range(8):
            a = l_s[zp, pl.ds(2 * cp, 40, stride=16), :]
            b = l_s[zp, pl.ds(2 * cp + 1, 40, stride=16), :]
            first = jnp.where(low, a, pltpu.roll(b, 64, 1))
            second = jnp.where(low, pltpu.roll(a, 64, 1), b)
            for z, val in ((2 * zp, first), (2 * zp + 1, second)):
                hi = val.astype(BF16).astype(F32)
                l2_s[z * 40 : (z + 1) * 40, cp * 128 : (cp + 1) * 128] = hi
                l3_s[z * 40 : (z + 1) * 40, cp * 128 : (cp + 1) * 128] = val - hi
    high_rows, low_rows = [
        ref[...].T.reshape(CH, 64, 240)[:, 0:56].reshape(CH * 56, 240).astype(BF16) for ref in (l2_s, l3_s)
    ]
    for i in range(8):
        one = one_ref[:, i * 256 : (i + 1) * 256]
        spread = jnp.dot(high_rows, one, preferred_element_type=F32)
        spread = spread + jnp.dot(low_rows, one, preferred_element_type=F32)
        spread = spread.reshape(CH, 56, 256) * h_ref[0:56, i * 256 : (i + 1) * 256][None]
        out_ref[0, 0, 0, :, i * 256 : (i + 1) * 256] = jnp.sum(spread, axis=1)


def call(kernel, outs, scratch, limit, flops, moved, in_specs=None):
    placed = {} if in_specs is None else {"in_specs": in_specs}
    return pl.pallas_call(
        kernel,
        out_shape=outs,
        **placed,
        scratch_shapes=scratch,
        compiler_params=pltpu.CompilerParams(vmem_limit_bytes=limit * MIB),
        cost_estimate=pl.CostEstimate(flops=flops, bytes_accessed=moved, transcendentals=0),
    )


def shape(dims, dtype):
    return jax.ShapeDtypeStruct(dims, dtype)


def swaps(axis):
    count = lax.axis_size(axis)
    inner = [(i, i ^ 1) for i in range(count)]
    outer = [(i, (i + (1 if i % 2 else -1)) % count) for i in range(count)]
    return inner, outer


def far_weights(off, table, far):
    vmem = pl.BlockSpec(memory_space=pltpu.VMEM)
    return call(
        table_kernel,
        (shape((SLOTS * 56, 128, 128), BF16), shape((56, 128, 128), BF16), shape((7, 128, 512), BF16)),
        [
            pltpu.VMEM((64 * 104, 128), F32),
            pltpu.VMEM((SLOTS * 56 * 136, 128), F32),
            pltpu.VMEM((SLOTS * 112, 256), BF16),
        ],
        24,
        2 * 49 * 5 * 112 * 256 * 256,
        10 * MIB,
        [vmem, pl.BlockSpec(memory_space=pltpu.SMEM), vmem],
    )(off, table, far)


def per_device(charges, positions, atom_cells, offsets, far_tables, upward_tables, downward_tables):
    up = jnp.pad(upward_tables.transpose(1, 0, 2), ((0, 15), (0, 0), (0, 15))).reshape(64, 512)
    up = jnp.concatenate([up, up], axis=0)
    down = jnp.pad(downward_tables, ((0, 0), (0, 15), (0, 15))).reshape(512, 64)
    blank = jnp.zeros_like(down)
    down = jnp.stack(
        [jnp.concatenate([down, blank], axis=1), jnp.concatenate([blank, down], axis=1)], axis=0
    )
    off = offsets.transpose(2, 0, 1).reshape(6, NOFF)
    far = far_tables.transpose(1, 2, 0, 3)
    coefs = jnp.asarray(COEFS)
    ztable = jnp.asarray(ZTABLE)
    cells = atom_cells.reshape(16, 128)
    swap = [(0, 1), (1, 0)]

    positions = pltpu.with_memory_space_constraint(positions.reshape(48, 128), pltpu.HBM)
    cells = pltpu.with_memory_space_constraint(cells, pltpu.HBM)
    leaf_z = call(
        poles_kernel,
        shape((1728, 128), BF16),
        [
            pltpu.VMEM((64, 2048), F32),
            pltpu.VMEM((240, 2048), BF16),
            pltpu.VMEM((16, 2048), BF16),
            pltpu.VMEM((48, 128), F32),
            pltpu.VMEM((16, 128), jnp.int32),
            pltpu.VMEM((1024, 128), F32),
            pltpu.VMEM((16, 2048), F32),
            pltpu.VMEM((1024, 2048), BF16),
            pltpu.VMEM((1024, 2048), BF16),
            pltpu.VMEM((3, 640, 128), F32),
            pltpu.SemaphoreType.DMA((3,)),
        ],
        20,
        2 * 2 * 256 * 2048 * 1024,
        2 * MIB,
        [pl.BlockSpec(memory_space=pltpu.HBM)] * 3,
    )(pltpu.with_memory_space_constraint(charges, pltpu.HBM), positions, cells)
    leaf_other = lax.ppermute(leaf_z, "gz", swap)
    part, pown = call(
        half_kernel,
        (shape((SLOTS, 576, 128), F32), shape((2, 144, 128), BF16)),
        [],
        8,
        1 << 27,
        2 * MIB,
    )(leaf_z, coefs, up)
    face = shape((848, 128), BF16)
    fb, fa, fo, po, pq = call(
        forward_kernel,
        (face, face, shape((SLOTS, 6, 2, 48, 128), BF16), shape((3, 48, 128), BF16), shape((3, 32, 128), BF16)),
        [pltpu.VMEM((4, 144, 128), BF16)],
        8,
        1 << 28,
        2 * MIB,
    )(part, pown, leaf_other, coefs, up)
    inner, outer = swaps("gx")
    fa = lax.ppermute(fa, "gx", inner)
    fb = lax.ppermute(fb, "gx", outer)
    fo, off = lax.optimization_barrier((fo, off))
    wl, wp, wq = far_weights(off, ztable, far)
    near = call(
        near_kernel,
        shape((SLOTS * 576, 256), F32),
        [pltpu.VMEM((SLOTS, 12, 2, 48, 128), BF16)],
        16,
        2 * 144 * 1792 * 256 * 12,
        8 * MIB,
    )(fo, wl)
    sb, sa, fh, edge, pown = call(
        far_kernel,
        (
            face,
            face,
            shape((SLOTS, 6, 2, 48, 128), BF16),
            shape((SLOTS * 192, 128), F32),
            shape((288, 128), F32),
        ),
        [
            pltpu.VMEM((SLOTS, 9, 2, 48, 128), BF16),
            pltpu.VMEM((1, 9, 2, 32, 128), BF16),
            pltpu.VMEM((9, 32, 128), BF16),
            pltpu.VMEM((2, SLOTS, 6, 3, 16, 128), F32),
            pltpu.VMEM((2, PSLOTS, 9, 16, 128), F32),
        ],
        16,
        2 * 288 * 1792 * 256 * 8,
        14 * MIB,
    )(fb, fa, near, po, pq, wl, wp, wq)
    inner, outer = swaps("gy")
    sa = lax.ppermute(sa, "gy", inner)
    sb = lax.ppermute(sb, "gy", outer)
    edge, positions, cells = lax.optimization_barrier((edge, positions, cells))
    own = call(
        inner_kernel,
        shape((1728, 128), F32),
        [pltpu.VMEM((SLOTS, 12, 2, 48, 128), BF16)],
        16,
        2 * 144 * 1792 * 256 * 12,
        8 * MIB,
    )(fo, fh, edge, wl)
    harm, one = call(
        atom_terms_kernel,
        (shape((64, 2048), F32), shape((240, 2048), BF16)),
        [pltpu.VMEM((1024, 128), F32)],
        8,
        1 << 24,
        2 * MIB,
    )(positions, cells)
    own, harm, one = lax.optimization_barrier((own, harm, one))
    full, zsend = call(
        join_kernel, (shape((2016, 128), F32), shape((2016, 128), BF16)), [], 8, 1 << 20, 3 * MIB
    )(own, pown, sb, sa)
    zrecv = lax.ppermute(zsend, "gz", swap)
    part, ppart = call(
        back_kernel,
        (shape((SLOTS, 576, 128), F32), shape((2, 144, 128), F32)),
        [],
        8,
        1 << 24,
        2 * MIB,
    )(full, coefs)
    potential = call(
        atoms_kernel,
        shape((1, 1, 1, CH, 2048), F32),
        [
            pltpu.VMEM((2, 144, 128), BF16),
            pltpu.VMEM((3, 144, 512), F32),
            pltpu.VMEM((3, 640, 128), F32),
            pltpu.VMEM((240, 1024), F32),
            pltpu.VMEM((240, 1024), F32),
        ],
        16,
        2 * 2 * 256 * 2048 * 1024,
        2 * MIB,
    )(part, ppart, zrecv, coefs, one, harm, down)
    return potential


def solution(mesh):
    placed = (
        P("gx", "gy", "gz", None, None),
        P("gx", "gy", "gz", None, None),
        P("gx", "gy", "gz", None),
        P(),
        P(),
        P(),
        P(),
    )
    return jax.shard_map(
        per_device,
        mesh=mesh,
        in_specs=placed,
        out_specs=P("gx", "gy", "gz", None, None),
        check_vma=False,
    )
```

```python
import math

import numpy as np
import jax
import jax.numpy as jnp
from jax import lax
from jax.experimental import pallas as pl
from jax.experimental.pallas import tpu as pltpu
from jax.sharding import PartitionSpec as P

CH = 16
ORDER = 6
TERMS = 49
NOFF = 128
SLOTS = 3
PSLOTS = 2
F32 = jnp.float32
BF16 = jnp.bfloat16
NT = (((1,), (1,)), ((), ()))
TN = (((0,), (0,)), ((), ()))
radial_scale = 1.6
MIB = 1 << 20


def spectral_constants():
    leaf_freq = [[None, 2, 4], [1, 3, 5]]
    pair_freq = [[2, 0], [1, 3]]
    turn = 2 * math.pi / 12
    pturn = 2 * math.pi / 6

    def fwd(core, s, ri, z):
        f = leaf_freq[core][s]
        if f is None:
            return float(z % 2 == ri)
        return math.cos(turn * f * z) if ri == 0 else -math.sin(turn * f * z)

    def inv(core, s, ri, z):
        f = leaf_freq[core][s]
        if f is None:
            return float(z % 2 == ri) / 6
        return (math.cos(turn * f * z) if ri == 0 else -math.sin(turn * f * z)) / 6

    def pfwd(core, s, ri, z):
        f = pair_freq[core][s]
        if s == 1:
            return math.cos(pturn * f * z) if ri == 0 else 0.0
        return math.cos(pturn * f * z) if ri == 0 else -math.sin(pturn * f * z)

    def pinv(core, s, ri, z):
        return pfwd(core, s, ri, z) / (6 if s == 1 else 3)

    halves = np.zeros((2, 104, 128))
    for core in range(2):
        row = 0

        def put(a, b):
            nonlocal row
            halves[core, row, :64] = a
            halves[core, row, 64:] = b
            row += 1

        for s in range(SLOTS):
            for v in range(6):
                z = (core if v < 3 else 1 - core) * 6 + 2 * (v % 3)
                put(fwd(core, s, 0, z), fwd(core, s, 1, z + 1))
                put(fwd(core, s, 0, z + 1), fwd(core, s, 1, z))
        for p in range(3):
            z = core * 6 + 2 * p
            for u in range(6):
                own = core if u < 3 else 1 - core
                s = u % 3
                put(inv(own, s, 0, z), inv(own, s, 1, z + 1))
                put(inv(own, s, 1, z), inv(own, s, 0, z + 1))
        for s in range(PSLOTS):
            for v in range(4):
                z = (core if v < 2 else 1 - core) * 3 + 2 * (v % 2)
                on = float(v % 2 == 0)
                put(pfwd(core, s, 0, z), on * pfwd(core, s, 1, z + 1))
                put(on * pfwd(core, s, 0, z + 1), pfwd(core, s, 1, z))
        for p in range(2):
            z = core * 3 + 2 * p
            on = float(p == 0)
            for u in range(4):
                own = core if u < 2 else 1 - core
                s = u % 2
                put(pinv(own, s, 0, z), on * pinv(own, s, 1, z + 1))
                put(pinv(own, s, 1, z), on * pinv(own, s, 0, z + 1))
        assert row == 104
    table = np.zeros((2, 80))
    for core in range(2):
        for pq in range(2):
            for s in range(SLOTS):
                f = leaf_freq[core][s]
                for d in range(7):
                    dz = d - 3
                    if f is None:
                        val = float(dz % 2 == pq)
                    else:
                        val = math.sin(turn * f * dz) if pq else math.cos(turn * f * dz)
                    table[core, (pq * SLOTS + s) * 7 + d] = val
            for s in range(PSLOTS):
                f = pair_freq[core][s]
                for d in range(7):
                    dz = d - 3
                    if s == 1:
                        val = 0.0 if pq else math.cos(pturn * f * dz)
                    else:
                        val = math.sin(pturn * f * dz) if pq else math.cos(pturn * f * dz)
                    table[core, 42 + (pq * PSLOTS + s) * 7 + d] = val
        table[core, 70] = 1.0 if core == 0 else -1.0
    return halves.astype(np.float32), table.reshape(-1).astype(np.float32)


COEFS, ZTABLE = spectral_constants()


def harmonic_terms(x, y, z):
    rsq = x * x + y * y + z * z
    cosines = {(0, 0): jnp.ones_like(x)}
    sines = {}
    for deg in range(1, ORDER + 1):
        for m in range(deg):
            inv = 1.0 / float((deg + m) * (deg - m))
            for part in (cosines, sines):
                if part is sines and m == 0:
                    continue
                val = ((2 * deg - 1) * inv) * (z * part[deg - 1, m])
                if m <= deg - 2:
                    val = val - inv * (rsq * part[deg - 2, m])
                part[deg, m] = val
        scale = -1.0 / (2.0 * deg)
        pc = cosines[deg - 1, deg - 1]
        if deg == 1:
            cosines[1, 1] = scale * x
            sines[1, 1] = scale * y
        else:
            ps = sines[deg - 1, deg - 1]
            cosines[deg, deg] = scale * (x * pc - y * ps)
            sines[deg, deg] = scale * (x * ps + y * pc)
    out = []
    for deg in range(ORDER + 1):
        out.append(cosines[deg, 0] * float(math.factorial(deg)))
        for m in range(1, deg + 1):
            factor = math.sqrt(math.factorial(deg + m) * math.factorial(deg - m))
            out.append(cosines[deg, m] * factor)
            out.append(sines[deg, m] * factor)
    return out


def low_lanes(rows):
    return lax.broadcasted_iota(jnp.int32, (rows, 128), 1) < 64


def cell_number_rows():
    row = lax.broadcasted_iota(jnp.int32, (256, 128), 0)
    z = jnp.zeros_like(row)
    for i in range(1, 6):
        z = z + (row >= 40 * i).astype(jnp.int32)
    xy = row - 40 * z
    return jnp.where(xy < 36, xy * 6 + z, -1)


def start_copies(pairs, sems):
    copies = [pltpu.make_async_copy(src, dst, sems.at[i]) for i, (src, dst) in enumerate(pairs)]
    for copy in copies:
        copy.start()
    return copies


def fill_harmonics(pos_s, h3_s, h_ref):
    terms = harmonic_terms(
        radial_scale * pos_s[0:16, :], radial_scale * pos_s[16:32, :], radial_scale * pos_s[32:48, :]
    )
    for k in range(TERMS):
        h3_s[k * 16 : (k + 1) * 16, :] = terms[k]
    h3_s[TERMS * 16 : 1024, :] = jnp.zeros((1024 - TERMS * 16, 128), F32)
    for i in range(16):
        h_ref[:, i * 128 : (i + 1) * 128] = h3_s[pl.ds(i, 64, stride=16), :]


def fill_onehot(cell_s, one_ref):
    number = cell_number_rows()
    for i in range(16):
        one_ref[:, i * 128 : (i + 1) * 128] = jnp.where(number == cell_s[i : i + 1, :], 1.0, 0.0).astype(BF16)


def atom_terms_kernel(pos_ref, cell_ref, h_ref, one_ref, h3_s):
    fill_harmonics(pos_ref, h3_s, h_ref)
    fill_onehot(cell_ref, one_ref)


def poles_kernel(ch_hbm, pos_hbm, cell_hbm, zs_ref, h_s, one_s, ch_s, pos_s, cell_s, h3_s, chf_s, w_s, f_s, sems):
    copies = start_copies(((pos_hbm, pos_s), (cell_hbm, cell_s), (ch_hbm.at[0, 0, 0], ch_s)), sems)
    copies[0].wait()
    fill_harmonics(pos_s, h3_s, h_s)
    copies[1].wait()
    fill_onehot(cell_s, one_s)
    copies[2].wait()
    chf_s[...] = ch_s[...].astype(F32)
    low = low_lanes(40)
    for n in range(4):
        for c in range(4 * n, 4 * n + 4):
            for i in range(4):
                sl = slice(i * 512, (i + 1) * 512)
                w = h_s[:, sl] * chf_s[c : c + 1, sl]
                hi = w.astype(BF16)
                w_s[c * 64 : (c + 1) * 64, sl] = hi
                w_s[c * 64 : (c + 1) * 64, 2048 + i * 512 : 2560 + i * 512] = (w - hi.astype(F32)).astype(BF16)
        rows = slice(n * 256, (n + 1) * 256)
        twice = jnp.concatenate([one_s[...], one_s[...]], axis=1)
        r = lax.dot_general(twice, w_s[rows, :], NT, preferred_element_type=F32)
        for half in range(2):
            c = n * 4 + half * 2
            for zp in range(3):
                a = r[zp * 80 : zp * 80 + 40, half * 128 : half * 128 + 128]
                b = r[zp * 80 + 40 : zp * 80 + 80, half * 128 : half * 128 + 128]
                f_s[zp, pl.ds(c, 40, stride=16), :] = jnp.where(low, a, pltpu.roll(b, 64, 1))
                f_s[zp, pl.ds(c + 1, 40, stride=16), :] = jnp.where(low, pltpu.roll(a, 64, 1), b)
    for zp in range(3):
        zs_ref[zp * 576 : (zp + 1) * 576, :] = f_s[zp, 0:576, :].astype(BF16)


def combine(values, coef, row):
    total = None
    for v, val in enumerate(values):
        part = val * coef(row + 2 * v) + pltpu.roll(val, 64, 1) * coef(row + 2 * v + 1)
        total = part if total is None else total + part
    return total


def lane_in_half(rows):
    return lax.broadcasted_iota(jnp.int32, (rows, 128), 1) & 63


def pack_three(firsts, seconds, thirds):
    lane = lane_in_half(16)
    outs_a, outs_b, pieces = [], [], []
    for i in range(3):
        outs_a.append(jnp.where(lane < TERMS, firsts[i], pltpu.roll(thirds[i], 49, 1)).astype(BF16))
        outs_b.append(jnp.where(lane < TERMS, seconds[i], pltpu.roll(thirds[i], 34, 1)).astype(BF16))
        pieces.append(pltpu.roll(thirds[i], (98, 117, 8)[i], 1))
    rest = jnp.where(lane < 19, pieces[0], jnp.where(lane < 38, pieces[1], pieces[2]))
    return outs_a, outs_b, rest.astype(BF16)


def unpack_third(first, second, rest, i):
    lane = lane_in_half(16)
    tail = pltpu.roll(rest, (30, 11, 120)[i], 1)
    return jnp.where(
        lane < 15, pltpu.roll(first, 79, 1), jnp.where(lane < 30, pltpu.roll(second, 94, 1), tail)
    )


def rest_shift(b):
    piece = b % 6
    return (64 * (piece // 3) + 19 * (piece % 3) - 30) % 128


def pack_parents(refs, firsts, seconds):
    lane = lax.broadcasted_iota(jnp.int32, (16, 128), 1)
    inner = lane & 63
    for b in range(9):
        spare = jnp.where(lane < 64, pltpu.roll(seconds[b], 49, 1), pltpu.roll(seconds[b], 98, 1))
        val = jnp.where(inner < TERMS, firsts[b], spare).astype(BF16)
        for ref in refs:
            ref[672 + b * 16 : 688 + b * 16, :] = val
    for i in range(2):
        pieces = [pltpu.roll(seconds[b], rest_shift(b), 1) for b in range(6 * i, min(6 * i + 6, 9))]
        halves = [
            jnp.where(inner < 19, part[0], jnp.where(inner < 38, part[1], part[2]))
            for part in (pieces[0:3], pieces[-3:])
        ]
        val = jnp.where(lane < 64, halves[0], halves[1]).astype(BF16)
        for ref in refs:
            ref[816 + i * 16 : 832 + i * 16, :] = val


def side_by_side(vals):
    low = low_lanes(16)
    first = jnp.where(low, vals[0], pltpu.roll(vals[2], 64, 1))
    return jnp.concatenate([first, jnp.where(low, vals[1], 0.0)], axis=0).astype(BF16)


def unpack_second(ref, b):
    lane = lax.broadcasted_iota(jnp.int32, (16, 128), 1)
    first = ref[672 + b * 16 : 688 + b * 16, :].astype(F32)
    rest = ref[816 + b // 6 * 16 : 832 + b // 6 * 16, :].astype(F32)
    tail = pltpu.roll(rest, (128 - rest_shift(b)) % 128, 1)
    return jnp.where(lane < 15, pltpu.roll(first, 79, 1), jnp.where(lane < 30, pltpu.roll(first, 30, 1), tail))


def parents_of(ref, up_ref):
    low = low_lanes(144)
    res = []
    for zp in range(3):
        split = ref[zp * 576 : (zp + 1) * 576, :].reshape(3, 2, 3, 2, 16, 128)
        lhs = jnp.concatenate(
            [split[:, p, :, q].reshape(144, 128) for p in range(2) for q in range(2)], axis=1
        )
        res.append(lax.dot_general(lhs, up_ref[...], NT, preferred_element_type=F32))
    return jnp.where(low, res[0], res[1]).astype(BF16), jnp.where(low, res[2], 0.0).astype(BF16)


def half_kernel(own_ref, coef_ref, up_ref, part_ref, pown_ref):
    core = lax.axis_index("gz")

    def coef(row):
        return coef_ref[core, row : row + 1, :]

    for b in range(36):
        values = [own_ref[zp * 576 + b * 16 : zp * 576 + b * 16 + 16, :].astype(F32) for zp in range(3)]
        for s in range(SLOTS):
            part_ref[s, b * 16 : b * 16 + 16, :] = combine(values, coef, s * 12)
    pown_ref[0], pown_ref[1] = parents_of(own_ref, up_ref)


def forward_kernel(part_ref, pown_ref, other_ref, coef_ref, up_ref, fb_ref, fa_ref, fo_ref, po_ref, pq_ref, pp_s):
    core = lax.axis_index("gz")
    odd = lax.rem(lax.axis_index("gx"), 2)

    def coef(row):
        return coef_ref[core, row : row + 1, :]

    for face, base in ((fa_ref, 3 - 3 * odd), (fb_ref, 3 * odd)):
        for xx in range(3):
            for par in range(2):
                done = [[], [], []]
                for spot in range(3):
                    at = pl.multiple_of(base * 96 + (xx * 6 + 2 * spot + par) * 16, 16)
                    values = [other_ref[pl.ds(at + zp * 576, 16), :].astype(F32) for zp in range(3)]
                    for s in range(SLOTS):
                        val = part_ref[s, pl.ds(at, 16), :] + combine(values, coef, s * 12 + 6)
                        done[s].append(val)
                        fo_ref[s, base + xx, par, spot * 16 : spot * 16 + 16, :] = val.astype(BF16)
                outs_a, outs_b, rest = pack_three(*done)
                block = xx * 2 + par
                for spot in range(3):
                    at = (block * 3 + spot) * 16
                    face[at : at + 16, :] = outs_a[spot]
                    face[288 + at : 304 + at, :] = outs_b[spot]
                face[576 + block * 16 : 592 + block * 16, :] = rest
    pp_s[0:2] = pown_ref[...]
    pp_s[2], pp_s[3] = parents_of(other_ref, up_ref)
    firsts, seconds = [], []
    for x in range(3):
        for pos in range(3):
            at = (x * 3 + (0, 2, 1)[pos]) * 16
            values = [pp_s[v, at : at + 16, :].astype(F32) for v in range(4)]
            firsts.append(combine(values, coef, 72))
            seconds.append(combine(values, coef, 80))
            po_ref[x, pos * 16 : pos * 16 + 16, :] = firsts[-1].astype(BF16)
        pq_ref[x] = side_by_side(seconds[3 * x : 3 * x + 3])
    pack_parents((fa_ref, fb_ref), firsts, seconds)


def table_kernel(off_ref, zt_ref, far_ref, wl_ref, wp_ref, wq_ref, t3_s, w_s, a_s):
    core = lax.axis_index("gz")
    base = core * 80

    def spread(j, carry):
        for k in range(TERMS):
            at = pl.multiple_of(j * 104, 8) + 2 * k
            t3_s[pl.ds(at, 2), :] = far_ref[j, k].astype(F32)
        return carry

    lax.fori_loop(0, TERMS, spread, 0)
    t3_s[TERMS * 104 : 64 * 104, :] = jnp.zeros((15 * 104, 128), F32)
    for level, slots, start, out_ref in ((0, SLOTS, 0, wl_ref), (1, PSLOTS, 42, wp_ref)):
        ox = off_ref[level : level + 1, :]
        oy = off_ref[2 + level : 3 + level, :]
        oz = off_ref[4 + level : 5 + level, :]
        code = (ox + 3) * 7 + (oy + 3)
        chosen = lax.broadcasted_iota(jnp.int32, (56, 128), 0) == code
        for q in range(2 * slots):
            row = jnp.zeros((1, 128), F32)
            for d in range(7):
                row = jnp.where(oz == d - 3, zt_ref[base + start + q * 7 + d], row)
            full = jnp.where(chosen, row, 0.0)
            hi = full.astype(BF16).astype(F32)
            a_s[q * 56 : (q + 1) * 56, 0:128] = hi.astype(BF16)
            a_s[q * 56 : (q + 1) * 56, 128:256] = (full - hi).astype(BF16)
        count = slots * 56
        low = low_lanes(count)
        block = lax.broadcasted_iota(jnp.int32, (count, 128), 0)
        sign = -1.0
        both = low
        if level == 0:
            sign = jnp.where(block < 56, zt_ref[base + 70], -1.0)
        else:
            both = low | (block >= 56)
        turned = 168 if level == 0 else 56

        def two_terms(i, carry):
            k = 2 * i
            rhs = []
            for e in range(2):
                tk = t3_s[pl.ds(2 * (k + e) + level, 64, stride=104), :].astype(BF16)
                wide = jnp.concatenate([tk, tk], axis=1)
                rhs += [wide, wide]
            out = lax.dot_general(
                a_s[0 : 2 * count, :], jnp.concatenate(rhs, axis=0), NT, preferred_element_type=F32
            )
            for e in range(2):
                even = out[0:count, e * 128 : (e + 1) * 128]
                odd = out[count : 2 * count, e * 128 : (e + 1) * 128]
                w_s[pl.ds(k + e, count, stride=136), :] = jnp.where(both, even, odd)
                w_s[pl.ds(k + e + 64, turned, stride=136), :] = jnp.where(low, sign * odd, even)[0:turned]
            return carry

        lax.fori_loop(0, 25, two_terms, 0, unroll=5)
        inner = lax.broadcasted_iota(jnp.int32, (128, 128), 0)
        filled = (inner & 63) < TERMS

        def one_block(b, carry):
            val = w_s[pl.ds(pl.multiple_of(b * 136, 8), 128), :]
            out_ref[b] = jnp.where(filled, val, 0.0).astype(BF16)
            return carry

        lax.fori_loop(0, turned, one_block, 0, unroll=4)
    half = low_lanes(64)
    kept = lax.broadcasted_iota(jnp.int32, (64, 128), 0) < TERMS

    def one_step(xi, carry):
        def block_of(dy):
            if dy < -3 or dy > 3:
                return jnp.zeros((64, 128), F32)
            return w_s[pl.ds(pl.multiple_of((56 + xi * 7 + dy + 3) * 136, 8), 64), :]

        for i in range(4):
            d = 2 * i - 3
            for p in range(2):
                val = jnp.where(half, block_of(d + p), block_of(d + p - 1))
                wq_ref[xi, p * 64 : p * 64 + 64, i * 128 : (i + 1) * 128] = jnp.where(kept, val, 0.0).astype(BF16)
        return carry

    lax.fori_loop(0, 7, one_step, 0)


def weight_tiles(weights, s, diff, steps):
    d = 2 * diff + 3
    zero = jnp.zeros((128, 128), BF16)

    def weight(xi, dy):
        if dy < -3 or dy > 3:
            return zero
        return weights[s * 56 + xi * 7 + dy + 3]

    return jnp.concatenate(
        [
            jnp.concatenate([weight(xi, d + p), weight(xi, d + p - 1)], axis=1)
            for xi in steps
            for p in range(2)
        ],
        axis=0,
    )


def field_rows(field, s, steps, first, xs, rows):
    return jnp.concatenate(
        [field[s, first + xi : first + xi + xs, p].reshape(rows, 128) for xi in steps for p in range(2)],
        axis=1,
    )


def share_out(accs, s, xs, pairs, ys, put):
    spots = (ys + 1) // 2
    for pair in range(pairs):
        for o in range(2):
            yo = 2 * pair - 3 + o
            if yo >= ys + 3:
                continue
            val = None
            for diff in range(-3, 1):
                spot = pair + diff
                if 0 <= spot < spots:
                    part = accs[diff + 3][:, spot, :, o * 128 : (o + 1) * 128]
                    val = part if val is None else val + part
            for x in range(xs):
                put(s, x, yo, val[x])


SENT = ((0, 0, 2), (-1, 0, 1), (-2, 2, 3), (-3, 1, 3))
KEPT = ((0, 2, 3), (-1, 1, 3), (-2, 0, 2), (-3, 0, 1))


def spot_rows(field, s, steps, xs, span):
    rows = xs * 16 * (span[1] - span[0])
    cut = slice(span[0] * 16, span[1] * 16)
    return jnp.concatenate(
        [field[s, xi : xi + xs, p, cut].reshape(rows, 128) for xi in steps for p in range(2)], axis=1
    )


def near_kernel(fo_ref, wl_ref, acc_ref, fl_s):
    zero = jnp.zeros((SLOTS, 3, 2, 48, 128), BF16)
    fl_s[:, 0:3] = zero
    fl_s[:, 9:12] = zero
    fl_s[:, 3:9] = fo_ref[...]
    at = 0
    for s in range(SLOTS):
        for diff, lo, hi in SENT:
            lhs = spot_rows(fl_s, s, range(7), 6, (lo, hi))
            size = 96 * (hi - lo)
            acc_ref[at : at + size, :] = jnp.dot(
                lhs, weight_tiles(wl_ref, s, diff, range(7)), preferred_element_type=F32
            )
            at += size


def inner_kernel(fo_ref, fh_ref, edge_ref, wl_ref, own_ref, fl_s):
    fl_s[:, 0:3] = fh_ref[:, 0:3]
    fl_s[:, 9:12] = fh_ref[:, 3:6]
    fl_s[:, 3:9] = fo_ref[...]
    for s in range(SLOTS):
        accs = {}
        for diff, lo, hi in KEPT:
            lhs = spot_rows(fl_s, s, range(7), 6, (lo, hi))
            acc = jnp.dot(lhs, weight_tiles(wl_ref, s, diff, range(7)), preferred_element_type=F32)
            acc = acc.reshape(6, hi - lo, 16, 256)
            for spot in range(lo, hi):
                accs[diff, spot] = acc[:, spot - lo]
        for pair in (2, 3):
            val = accs[-pair, 0] + accs[1 - pair, 1] + accs[2 - pair, 2]
            for x in range(6):
                for o in range(2):
                    at = ((s * 6 + x) * 6 + 2 * pair - 3 + o) * 16
                    own_ref[at : at + 16, :] = val[x, :, o * 128 : (o + 1) * 128]
        for x in range(6):
            at = (s * 6 + x) * 96
            edge = (s * 6 + x) * 32
            own_ref[at : at + 16, :] = edge_ref[edge : edge + 16, :]
            own_ref[at + 80 : at + 96, :] = edge_ref[edge + 16 : edge + 32, :]


def far_kernel(
    b_ref, a_ref, acc_ref, po_ref, pq_ref, wl_ref, wp_ref, wq_ref,
    sb_ref, sa_ref, fh_ref, edge_ref, pown_ref, fl_s, fp_s, fq_s, ex_s, px_s
):
    xodd = lax.rem(lax.axis_index("gx"), 2)
    yodd = lax.rem(lax.axis_index("gy"), 2)
    fl_s[:, 3:6] = jnp.zeros((SLOTS, 3, 2, 48, 128), BF16)
    fp_s[0, :, 1, 16:32] = jnp.zeros((9, 16, 128), BF16)
    part = po_ref[...]
    fp_s[0, 3:6, 0] = part[:, 0:32]
    fp_s[0, 3:6, 1, 0:16] = part[:, 32:48]
    fq_s[3:6] = pq_ref[...]
    for ref, far_side in ((a_ref, 1 - xodd), (b_ref, xodd)):
        for x in range(3):
            for par in range(2):
                block = x * 2 + par
                rest = ref[576 + block * 16 : 592 + block * 16, :].astype(F32)
                for spot in range(3):
                    at = (block * 3 + spot) * 16
                    one = ref[at : at + 16, :]
                    two = ref[288 + at : 304 + at, :]
                    three = unpack_third(one.astype(F32), two.astype(F32), rest, spot)
                    for s, val in enumerate((one, two, three.astype(BF16))):
                        fl_s[s, far_side * 6 + x, par, spot * 16 : spot * 16 + 16, :] = val
                        fh_ref[s, far_side * 3 + x, par, spot * 16 : spot * 16 + 16, :] = val
            for pos in range(3):
                b = x * 3 + pos
                at = (pos % 2) * 16
                fp_s[0, far_side * 6 + x, pos // 2, at : at + 16] = ref[672 + b * 16 : 688 + b * 16, :]
            fq_s[far_side * 6 + x] = side_by_side([unpack_second(ref, x * 3 + pos) for pos in range(3)])

    def parent_put(s, x, yo, val):
        if 0 <= yo < 3:
            at = ((s * 3 + x) * 3 + yo) * 16
            pown_ref[at : at + 16, :] = val
        else:
            px_s[0 if yo < 0 else 1, s, x * 3 + (yo + 3 if yo < 0 else yo - 3)] = val

    row = 0
    for s in range(SLOTS):
        accs = {}
        for diff, lo, hi in SENT:
            half = 48 * (hi - lo)
            for i, steps in enumerate((range(3), range(4, 7))):
                lhs = spot_rows(fl_s, s, steps, 3, (lo, hi))
                acc = acc_ref[row : row + half, :] + jnp.dot(
                    lhs, weight_tiles(wl_ref, s, diff, steps), preferred_element_type=F32
                )
                row += half
                acc = acc.reshape(3, hi - lo, 16, 256)
                for spot in range(lo, hi):
                    for x in range(3):
                        accs[diff, spot, 3 * i + x] = acc[x, spot - lo]
        for x in range(6):
            low = accs[0, 0, x]
            low_next = accs[-1, 0, x] + accs[0, 1, x]
            high_next = accs[-3, 1, x] + accs[-2, 2, x]
            high = accs[-3, 2, x]
            ex_s[0, s, x, 0] = low[:, 0:128]
            ex_s[0, s, x, 1] = low[:, 128:256]
            ex_s[0, s, x, 2] = low_next[:, 0:128]
            ex_s[1, s, x, 0] = high_next[:, 128:256]
            ex_s[1, s, x, 1] = high[:, 0:128]
            ex_s[1, s, x, 2] = high[:, 128:256]
            edge = (s * 6 + x) * 32
            edge_ref[edge : edge + 16, :] = low_next[:, 128:256]
            edge_ref[edge + 16 : edge + 32, :] = high_next[:, 0:128]
    lhs = field_rows(fp_s, 0, range(7), 0, 3, 96)
    accs = [
        jnp.dot(lhs, weight_tiles(wp_ref, 0, diff, range(7)), preferred_element_type=F32).reshape(3, 2, 16, 256)
        for diff in range(-3, 1)
    ]
    share_out(accs, 0, 3, 5, 3, parent_put)
    lhs = jnp.concatenate([fq_s[xi : xi + 3].reshape(96, 128) for xi in range(7)], axis=1)
    acc = jnp.dot(lhs, wq_ref[...].reshape(896, 512), preferred_element_type=F32).reshape(3, 2, 16, 512)
    for pair in range(5):
        val = None
        for diff in range(-3, 1):
            spot = pair + diff
            if 0 <= spot < 2:
                piece = acc[:, spot, :, (diff + 3) * 128 : (diff + 4) * 128]
                val = piece if val is None else val + piece
        for x in range(3):
            parent_put(1, x, 2 * pair - 3, val[x])
            if pair < 4:
                parent_put(1, x, 2 * pair - 2, pltpu.roll(val[x], 64, 1))
    for side, ref in ((1 - yodd, sa_ref), (yodd, sb_ref)):
        for x in range(6):
            outs_a, outs_b, rest = pack_three(
                *[[ex_s[side, s, x, i] for i in range(3)] for s in range(SLOTS)]
            )
            for i in range(3):
                at = (x * 3 + i) * 16
                ref[at : at + 16, :] = outs_a[i]
                ref[288 + at : 304 + at, :] = outs_b[i]
            ref[576 + x * 16 : 592 + x * 16, :] = rest
        pack_parents((ref,), *[[px_s[side, s, b] for b in range(9)] for s in range(PSLOTS)])


def join_kernel(own_ref, pown_ref, b_ref, a_ref, full_ref, zs_ref):
    yodd = lax.rem(lax.axis_index("gy"), 2)
    for ref, upper in ((a_ref, 1 - yodd), (b_ref, yodd)):
        for x in range(6):
            rest = ref[576 + x * 16 : 592 + x * 16, :].astype(F32)
            for i in range(3):
                at = (x * 3 + i) * 16
                one = ref[at : at + 16, :].astype(F32)
                two = ref[288 + at : 304 + at, :].astype(F32)
                three = unpack_third(one, two, rest, i)
                for s, val in enumerate((one, two, three)):
                    row = pl.multiple_of(((s * 6 + x) * 6 + i) * 16 + upper * 48, 16)
                    total = own_ref[pl.ds(row, 16), :] + val
                    full_ref[pl.ds(row, 16), :] = total
                    zs_ref[pl.ds(row, 16), :] = total.astype(BF16)
    for b in range(9):
        for s in range(PSLOTS):
            row = 1728 + (s * 9 + b) * 16
            total = pown_ref[row - 1728 : row - 1712, :]
            for ref in (a_ref, b_ref):
                if s == 0:
                    total = total + ref[672 + b * 16 : 688 + b * 16, :].astype(F32)
                else:
                    total = total + unpack_second(ref, b)
            full_ref[row : row + 16, :] = total
            zs_ref[row : row + 16, :] = total.astype(BF16)


def back_kernel(own_ref, coef_ref, part_ref, ppart_ref):
    core = lax.axis_index("gz")

    def coef(row):
        return coef_ref[core, row : row + 1, :]

    for i in range(9):
        at = 1728 + i * 16
        values = [own_ref[at + s * 144 : at + s * 144 + 16, :] for s in range(PSLOTS)]
        for p in range(2):
            ppart_ref[p, i * 16 : (i + 1) * 16, :] = combine(values, coef, 88 + p * 8)
    for b in range(36):
        values = [own_ref[s * 576 + b * 16 : s * 576 + b * 16 + 16, :] for s in range(SLOTS)]
        for zp in range(3):
            part_ref[zp, b * 16 : b * 16 + 16, :] = combine(values, coef, 36 + zp * 12)


def atoms_kernel(part_ref, ppart_ref, other_ref, coef_ref, one_ref, h_ref, down_ref, out_ref, pf_s, lift_s, l_s, l2_s, l3_s):
    core = lax.axis_index("gz")

    def coef(row):
        return coef_ref[core, row : row + 1, :]

    for i in range(9):
        at = 1728 + i * 16
        values = [other_ref[at + s * 144 : at + s * 144 + 16, :].astype(F32) for s in range(PSLOTS)]
        for p in range(2):
            total = ppart_ref[p, i * 16 : (i + 1) * 16, :] + combine(values, coef, 92 + p * 8)
            hi = total.astype(BF16)
            pf_s[p, i * 16 : (i + 1) * 16, 0:128] = hi
            pf_s[p, i * 16 : (i + 1) * 16, 128:256] = (total - hi.astype(F32)).astype(BF16)
    for k in range(3):
        table = jnp.concatenate([down_ref[k % 2], down_ref[k % 2]], axis=1)
        lift_s[k] = lax.dot_general(pf_s[k // 2], table, NT, preferred_element_type=F32)
    for x in range(6):
        for y in range(6):
            at = (x * 6 + y) * 16
            values = [other_ref[s * 576 + at : s * 576 + at + 16, :].astype(F32) for s in range(SLOTS)]
            par = ((x // 2) * 3 + y // 2) * 16
            lane = ((x % 2) * 2 + y % 2) * 128
            for zp in range(3):
                l_s[zp, at : at + 16, :] = (
                    part_ref[zp, at : at + 16, :]
                    + combine(values, coef, 42 + zp * 12)
                    + lift_s[zp, par : par + 16, lane : lane + 128]
                )
    low = low_lanes(40)
    for zp in range(3):
        l_s[zp, 576:640, :] = jnp.zeros((64, 128), F32)
        for cp in range(8):
            a = l_s[zp, pl.ds(2 * cp, 40, stride=16), :]
            b = l_s[zp, pl.ds(2 * cp + 1, 40, stride=16), :]
            first = jnp.where(low, a, pltpu.roll(b, 64, 1))
            second = jnp.where(low, pltpu.roll(a, 64, 1), b)
            for z, val in ((2 * zp, first), (2 * zp + 1, second)):
                hi = val.astype(BF16).astype(F32)
                l2_s[z * 40 : (z + 1) * 40, cp * 128 : (cp + 1) * 128] = hi
                l3_s[z * 40 : (z + 1) * 40, cp * 128 : (cp + 1) * 128] = val - hi
    for ref in (l2_s, l3_s):
        ref[240:256, :] = jnp.zeros((16, 1024), F32)
    rows = jnp.concatenate(
        [
            ref[...].T.reshape(CH, 64, 256)[:, 0:56].reshape(CH * 56, 256).astype(BF16)
            for ref in (l2_s, l3_s)
        ],
        axis=1,
    )
    for i in range(8):
        one = one_ref[:, i * 256 : (i + 1) * 256]
        spread = jnp.dot(rows, jnp.concatenate([one, one], axis=0), preferred_element_type=F32)
        spread = spread.reshape(CH, 56, 256) * h_ref[0:56, i * 256 : (i + 1) * 256][None]
        out_ref[0, 0, 0, :, i * 256 : (i + 1) * 256] = jnp.sum(spread, axis=1)


def call(kernel, outs, scratch, limit, flops, moved, in_specs=None):
    placed = {} if in_specs is None else {"in_specs": in_specs}
    return pl.pallas_call(
        kernel,
        out_shape=outs,
        **placed,
        scratch_shapes=scratch,
        compiler_params=pltpu.CompilerParams(vmem_limit_bytes=limit * MIB),
        cost_estimate=pl.CostEstimate(flops=flops, bytes_accessed=moved, transcendentals=0),
    )


def shape(dims, dtype):
    return jax.ShapeDtypeStruct(dims, dtype)


def swaps(axis):
    count = lax.axis_size(axis)
    inner = [(i, i ^ 1) for i in range(count)]
    outer = [(i, (i + (1 if i % 2 else -1)) % count) for i in range(count)]
    return inner, outer


def far_weights(off, table, far):
    vmem = pl.BlockSpec(memory_space=pltpu.VMEM)
    return call(
        table_kernel,
        (shape((SLOTS * 56, 128, 128), BF16), shape((56, 128, 128), BF16), shape((7, 128, 512), BF16)),
        [
            pltpu.VMEM((64 * 104, 128), F32),
            pltpu.VMEM((SLOTS * 56 * 136, 128), F32),
            pltpu.VMEM((SLOTS * 112, 256), BF16),
        ],
        24,
        2 * 49 * 5 * 112 * 256 * 256,
        10 * MIB,
        [vmem, pl.BlockSpec(memory_space=pltpu.SMEM), vmem],
    )(off, table, far)


def per_device(charges, positions, atom_cells, offsets, far_tables, upward_tables, downward_tables):
    up = jnp.pad(upward_tables.transpose(1, 0, 2), ((0, 15), (0, 0), (0, 15))).reshape(64, 512)
    up = jnp.concatenate([up, up], axis=0)
    down = jnp.pad(downward_tables, ((0, 0), (0, 15), (0, 15))).reshape(512, 64)
    blank = jnp.zeros_like(down)
    down = jnp.stack(
        [jnp.concatenate([down, blank], axis=1), jnp.concatenate([blank, down], axis=1)], axis=0
    )
    off = offsets.transpose(2, 0, 1).reshape(6, NOFF)
    far = far_tables.transpose(1, 2, 0, 3)
    coefs = jnp.asarray(COEFS)
    ztable = jnp.asarray(ZTABLE)
    cells = atom_cells.reshape(16, 128)
    swap = [(0, 1), (1, 0)]

    positions = pltpu.with_memory_space_constraint(positions.reshape(48, 128), pltpu.HBM)
    cells = pltpu.with_memory_space_constraint(cells, pltpu.HBM)
    leaf_z = call(
        poles_kernel,
        shape((1728, 128), BF16),
        [
            pltpu.VMEM((64, 2048), F32),
            pltpu.VMEM((256, 2048), BF16),
            pltpu.VMEM((16, 2048), BF16),
            pltpu.VMEM((48, 128), F32),
            pltpu.VMEM((16, 128), jnp.int32),
            pltpu.VMEM((1024, 128), F32),
            pltpu.VMEM((16, 2048), F32),
            pltpu.VMEM((1024, 4096), BF16),
            pltpu.VMEM((3, 640, 128), F32),
            pltpu.SemaphoreType.DMA((3,)),
        ],
        20,
        2 * 2 * 256 * 2048 * 1024,
        2 * MIB,
        [pl.BlockSpec(memory_space=pltpu.HBM)] * 3,
    )(pltpu.with_memory_space_constraint(charges, pltpu.HBM), positions, cells)
    leaf_other = lax.ppermute(leaf_z, "gz", swap)
    part, pown = call(
        half_kernel,
        (shape((SLOTS, 576, 128), F32), shape((2, 144, 128), BF16)),
        [],
        8,
        1 << 27,
        2 * MIB,
    )(leaf_z, coefs, up)
    face = shape((848, 128), BF16)
    fb, fa, fo, po, pq = call(
        forward_kernel,
        (face, face, shape((SLOTS, 6, 2, 48, 128), BF16), shape((3, 48, 128), BF16), shape((3, 32, 128), BF16)),
        [pltpu.VMEM((4, 144, 128), BF16)],
        8,
        1 << 28,
        2 * MIB,
    )(part, pown, leaf_other, coefs, up)
    inner, outer = swaps("gx")
    fa = lax.ppermute(fa, "gx", inner)
    fb = lax.ppermute(fb, "gx", outer)
    fo, off = lax.optimization_barrier((fo, off))
    wl, wp, wq = far_weights(off, ztable, far)
    near = call(
        near_kernel,
        shape((SLOTS * 576, 256), F32),
        [pltpu.VMEM((SLOTS, 12, 2, 48, 128), BF16)],
        16,
        2 * 144 * 1792 * 256 * 12,
        8 * MIB,
    )(fo, wl)
    sb, sa, fh, edge, pown = call(
        far_kernel,
        (
            face,
            face,
            shape((SLOTS, 6, 2, 48, 128), BF16),
            shape((SLOTS * 192, 128), F32),
            shape((288, 128), F32),
        ),
        [
            pltpu.VMEM((SLOTS, 9, 2, 48, 128), BF16),
            pltpu.VMEM((1, 9, 2, 32, 128), BF16),
            pltpu.VMEM((9, 32, 128), BF16),
            pltpu.VMEM((2, SLOTS, 6, 3, 16, 128), F32),
            pltpu.VMEM((2, PSLOTS, 9, 16, 128), F32),
        ],
        16,
        2 * 288 * 1792 * 256 * 8,
        14 * MIB,
    )(fb, fa, near, po, pq, wl, wp, wq)
    inner, outer = swaps("gy")
    sa = lax.ppermute(sa, "gy", inner)
    sb = lax.ppermute(sb, "gy", outer)
    edge, positions, cells = lax.optimization_barrier((edge, positions, cells))
    own = call(
        inner_kernel,
        shape((1728, 128), F32),
        [pltpu.VMEM((SLOTS, 12, 2, 48, 128), BF16)],
        16,
        2 * 144 * 1792 * 256 * 12,
        8 * MIB,
    )(fo, fh, edge, wl)
    harm, one = call(
        atom_terms_kernel,
        (shape((64, 2048), F32), shape((256, 2048), BF16)),
        [pltpu.VMEM((1024, 128), F32)],
        8,
        1 << 24,
        2 * MIB,
    )(positions, cells)
    own, harm, one = lax.optimization_barrier((own, harm, one))
    full, zsend = call(
        join_kernel, (shape((2016, 128), F32), shape((2016, 128), BF16)), [], 8, 1 << 20, 3 * MIB
    )(own, pown, sb, sa)
    zrecv = lax.ppermute(zsend, "gz", swap)
    part, ppart = call(
        back_kernel,
        (shape((SLOTS, 576, 128), F32), shape((2, 144, 128), F32)),
        [],
        8,
        1 << 24,
        2 * MIB,
    )(full, coefs)
    potential = call(
        atoms_kernel,
        shape((1, 1, 1, CH, 2048), F32),
        [
            pltpu.VMEM((2, 144, 256), BF16),
            pltpu.VMEM((3, 144, 512), F32),
            pltpu.VMEM((3, 640, 128), F32),
            pltpu.VMEM((256, 1024), F32),
            pltpu.VMEM((256, 1024), F32),
        ],
        16,
        2 * 2 * 256 * 2048 * 1024,
        2 * MIB,
    )(part, ppart, zrecv, coefs, one, harm, down)
    return potential


def solution(mesh):
    placed = (
        P("gx", "gy", "gz", None, None),
        P("gx", "gy", "gz", None, None),
        P("gx", "gy", "gz", None),
        P(),
        P(),
        P(),
        P(),
    )
    return jax.shard_map(
        per_device,
        mesh=mesh,
        in_specs=placed,
        out_specs=P("gx", "gy", "gz", None, None),
        check_vma=False,
    )
```

```python
import math

import numpy as np
import jax
import jax.numpy as jnp
from jax import lax
from jax.experimental import pallas as pl
from jax.experimental.pallas import tpu as pltpu
from jax.sharding import PartitionSpec as P

CH = 16
ORDER = 6
TERMS = 49
NOFF = 128
SLOTS = 3
PSLOTS = 2
F32 = jnp.float32
BF16 = jnp.bfloat16
NT = (((1,), (1,)), ((), ()))
TN = (((0,), (0,)), ((), ()))
radial_scale = 1.6
MIB = 1 << 20


def spectral_constants():
    leaf_freq = [[None, 2, 4], [1, 3, 5]]
    pair_freq = [[2, 0], [1, 3]]
    turn = 2 * math.pi / 12
    pturn = 2 * math.pi / 6

    def fwd(core, s, ri, z):
        f = leaf_freq[core][s]
        if f is None:
            return float(z % 2 == ri)
        return math.cos(turn * f * z) if ri == 0 else -math.sin(turn * f * z)

    def inv(core, s, ri, z):
        f = leaf_freq[core][s]
        if f is None:
            return float(z % 2 == ri) / 6
        return (math.cos(turn * f * z) if ri == 0 else -math.sin(turn * f * z)) / 6

    def pfwd(core, s, ri, z):
        f = pair_freq[core][s]
        if s == 1:
            return math.cos(pturn * f * z) if ri == 0 else 0.0
        return math.cos(pturn * f * z) if ri == 0 else -math.sin(pturn * f * z)

    def pinv(core, s, ri, z):
        return pfwd(core, s, ri, z) / (6 if s == 1 else 3)

    halves = np.zeros((2, 104, 128))
    for core in range(2):
        row = 0

        def put(a, b):
            nonlocal row
            halves[core, row, :64] = a
            halves[core, row, 64:] = b
            row += 1

        for s in range(SLOTS):
            for v in range(6):
                z = (core if v < 3 else 1 - core) * 6 + 2 * (v % 3)
                put(fwd(core, s, 0, z), fwd(core, s, 1, z + 1))
                put(fwd(core, s, 0, z + 1), fwd(core, s, 1, z))
        for p in range(3):
            z = core * 6 + 2 * p
            for u in range(6):
                own = core if u < 3 else 1 - core
                s = u % 3
                put(inv(own, s, 0, z), inv(own, s, 1, z + 1))
                put(inv(own, s, 1, z), inv(own, s, 0, z + 1))
        for s in range(PSLOTS):
            for v in range(4):
                z = (core if v < 2 else 1 - core) * 3 + 2 * (v % 2)
                on = float(v % 2 == 0)
                put(pfwd(core, s, 0, z), on * pfwd(core, s, 1, z + 1))
                put(on * pfwd(core, s, 0, z + 1), pfwd(core, s, 1, z))
        for p in range(2):
            z = core * 3 + 2 * p
            on = float(p == 0)
            for u in range(4):
                own = core if u < 2 else 1 - core
                s = u % 2
                put(pinv(own, s, 0, z), on * pinv(own, s, 1, z + 1))
                put(pinv(own, s, 1, z), on * pinv(own, s, 0, z + 1))
        assert row == 104
    table = np.zeros((2, 80))
    for core in range(2):
        for pq in range(2):
            for s in range(SLOTS):
                f = leaf_freq[core][s]
                for d in range(7):
                    dz = d - 3
                    if f is None:
                        val = float(dz % 2 == pq)
                    else:
                        val = math.sin(turn * f * dz) if pq else math.cos(turn * f * dz)
                    table[core, (pq * SLOTS + s) * 7 + d] = val
            for s in range(PSLOTS):
                f = pair_freq[core][s]
                for d in range(7):
                    dz = d - 3
                    if s == 1:
                        val = 0.0 if pq else math.cos(pturn * f * dz)
                    else:
                        val = math.sin(pturn * f * dz) if pq else math.cos(pturn * f * dz)
                    table[core, 42 + (pq * PSLOTS + s) * 7 + d] = val
        table[core, 70] = 1.0 if core == 0 else -1.0
    return halves.astype(np.float32), table.reshape(-1).astype(np.float32)


COEFS, ZTABLE = spectral_constants()


def harmonic_terms(x, y, z):
    rsq = x * x + y * y + z * z
    cosines = {(0, 0): jnp.ones_like(x)}
    sines = {}
    for deg in range(1, ORDER + 1):
        for m in range(deg):
            inv = 1.0 / float((deg + m) * (deg - m))
            for part in (cosines, sines):
                if part is sines and m == 0:
                    continue
                val = ((2 * deg - 1) * inv) * (z * part[deg - 1, m])
                if m <= deg - 2:
                    val = val - inv * (rsq * part[deg - 2, m])
                part[deg, m] = val
        scale = -1.0 / (2.0 * deg)
        pc = cosines[deg - 1, deg - 1]
        if deg == 1:
            cosines[1, 1] = scale * x
            sines[1, 1] = scale * y
        else:
            ps = sines[deg - 1, deg - 1]
            cosines[deg, deg] = scale * (x * pc - y * ps)
            sines[deg, deg] = scale * (x * ps + y * pc)
    out = []
    for deg in range(ORDER + 1):
        out.append(cosines[deg, 0] * float(math.factorial(deg)))
        for m in range(1, deg + 1):
            factor = math.sqrt(math.factorial(deg + m) * math.factorial(deg - m))
            out.append(cosines[deg, m] * factor)
            out.append(sines[deg, m] * factor)
    return out


def low_lanes(rows):
    return lax.broadcasted_iota(jnp.int32, (rows, 128), 1) < 64


def cell_number_rows():
    row = lax.broadcasted_iota(jnp.int32, (256, 128), 0)
    z = jnp.zeros_like(row)
    for i in range(1, 6):
        z = z + (row >= 40 * i).astype(jnp.int32)
    xy = row - 40 * z
    return jnp.where(xy < 36, xy * 6 + z, -1)


def start_copies(pairs, sems):
    copies = [pltpu.make_async_copy(src, dst, sems.at[i]) for i, (src, dst) in enumerate(pairs)]
    for copy in copies:
        copy.start()
    return copies


def fill_harmonics(pos_s, h3_s, h_ref):
    terms = harmonic_terms(
        radial_scale * pos_s[0:16, :], radial_scale * pos_s[16:32, :], radial_scale * pos_s[32:48, :]
    )
    for k in range(TERMS):
        h3_s[k * 16 : (k + 1) * 16, :] = terms[k]
    h3_s[TERMS * 16 : 1024, :] = jnp.zeros((1024 - TERMS * 16, 128), F32)
    for i in range(16):
        h_ref[:, i * 128 : (i + 1) * 128] = h3_s[pl.ds(i, 64, stride=16), :]


def fill_onehot(cell_s, one_ref):
    number = cell_number_rows()
    for i in range(16):
        one_ref[:, i * 128 : (i + 1) * 128] = jnp.where(number == cell_s[i : i + 1, :], 1.0, 0.0).astype(BF16)


def atom_terms_kernel(pos_ref, cell_ref, h_ref, one_ref, h3_s):
    fill_harmonics(pos_ref, h3_s, h_ref)
    fill_onehot(cell_ref, one_ref)


def poles_kernel(ch_hbm, pos_hbm, cell_hbm, zs_ref, h_s, one_s, ch_s, pos_s, cell_s, h3_s, chf_s, w_s, f_s, sems):
    copies = start_copies(((pos_hbm, pos_s), (cell_hbm, cell_s), (ch_hbm.at[0, 0, 0], ch_s)), sems)
    copies[0].wait()
    fill_harmonics(pos_s, h3_s, h_s)
    copies[1].wait()
    fill_onehot(cell_s, one_s)
    copies[2].wait()
    chf_s[...] = ch_s[...].astype(F32)
    low = low_lanes(40)
    for n in range(4):
        for c in range(4 * n, 4 * n + 4):
            for i in range(4):
                sl = slice(i * 512, (i + 1) * 512)
                w = h_s[:, sl] * chf_s[c : c + 1, sl]
                hi = w.astype(BF16)
                w_s[c * 64 : (c + 1) * 64, sl] = hi
                w_s[c * 64 : (c + 1) * 64, 2048 + i * 512 : 2560 + i * 512] = (w - hi.astype(F32)).astype(BF16)
        rows = slice(n * 256, (n + 1) * 256)
        twice = jnp.concatenate([one_s[...], one_s[...]], axis=1)
        r = lax.dot_general(twice, w_s[rows, :], NT, preferred_element_type=F32)
        for half in range(2):
            c = n * 4 + half * 2
            for zp in range(3):
                a = r[zp * 80 : zp * 80 + 40, half * 128 : half * 128 + 128]
                b = r[zp * 80 + 40 : zp * 80 + 80, half * 128 : half * 128 + 128]
                f_s[zp, pl.ds(c, 40, stride=16), :] = jnp.where(low, a, pltpu.roll(b, 64, 1))
                f_s[zp, pl.ds(c + 1, 40, stride=16), :] = jnp.where(low, pltpu.roll(a, 64, 1), b)
    for zp in range(3):
        zs_ref[zp * 576 : (zp + 1) * 576, :] = f_s[zp, 0:576, :].astype(BF16)


def combine(values, coef, row):
    total = None
    for v, val in enumerate(values):
        part = val * coef(row + 2 * v) + pltpu.roll(val, 64, 1) * coef(row + 2 * v + 1)
        total = part if total is None else total + part
    return total


def lane_in_half(rows):
    return lax.broadcasted_iota(jnp.int32, (rows, 128), 1) & 63


def pack_three(firsts, seconds, thirds):
    lane = lane_in_half(16)
    outs_a, outs_b, pieces = [], [], []
    for i in range(3):
        outs_a.append(jnp.where(lane < TERMS, firsts[i], pltpu.roll(thirds[i], 49, 1)).astype(BF16))
        outs_b.append(jnp.where(lane < TERMS, seconds[i], pltpu.roll(thirds[i], 34, 1)).astype(BF16))
        pieces.append(pltpu.roll(thirds[i], (98, 117, 8)[i], 1))
    rest = jnp.where(lane < 19, pieces[0], jnp.where(lane < 38, pieces[1], pieces[2]))
    return outs_a, outs_b, rest.astype(BF16)


def unpack_third(first, second, rest, i):
    lane = lane_in_half(16)
    tail = pltpu.roll(rest, (30, 11, 120)[i], 1)
    return jnp.where(
        lane < 15, pltpu.roll(first, 79, 1), jnp.where(lane < 30, pltpu.roll(second, 94, 1), tail)
    )


def rest_shift(b):
    piece = b % 6
    return (64 * (piece // 3) + 19 * (piece % 3) - 30) % 128


def pack_parents(refs, firsts, seconds):
    lane = lax.broadcasted_iota(jnp.int32, (16, 128), 1)
    inner = lane & 63
    for b in range(9):
        spare = jnp.where(lane < 64, pltpu.roll(seconds[b], 49, 1), pltpu.roll(seconds[b], 98, 1))
        val = jnp.where(inner < TERMS, firsts[b], spare).astype(BF16)
        for ref in refs:
            ref[672 + b * 16 : 688 + b * 16, :] = val
    for i in range(2):
        pieces = [pltpu.roll(seconds[b], rest_shift(b), 1) for b in range(6 * i, min(6 * i + 6, 9))]
        halves = [
            jnp.where(inner < 19, part[0], jnp.where(inner < 38, part[1], part[2]))
            for part in (pieces[0:3], pieces[-3:])
        ]
        val = jnp.where(lane < 64, halves[0], halves[1]).astype(BF16)
        for ref in refs:
            ref[816 + i * 16 : 832 + i * 16, :] = val


def side_by_side(vals):
    low = low_lanes(16)
    first = jnp.where(low, vals[0], pltpu.roll(vals[2], 64, 1))
    return jnp.concatenate([first, jnp.where(low, vals[1], 0.0)], axis=0).astype(BF16)


def unpack_second(ref, b):
    lane = lax.broadcasted_iota(jnp.int32, (16, 128), 1)
    first = ref[672 + b * 16 : 688 + b * 16, :].astype(F32)
    rest = ref[816 + b // 6 * 16 : 832 + b // 6 * 16, :].astype(F32)
    tail = pltpu.roll(rest, (128 - rest_shift(b)) % 128, 1)
    return jnp.where(lane < 15, pltpu.roll(first, 79, 1), jnp.where(lane < 30, pltpu.roll(first, 30, 1), tail))


def parents_of(ref, up_ref):
    low = low_lanes(144)
    res = []
    for zp in range(3):
        split = ref[zp * 576 : (zp + 1) * 576, :].reshape(3, 2, 3, 2, 16, 128)
        lhs = jnp.concatenate(
            [split[:, p, :, q].reshape(144, 128) for p in range(2) for q in range(2)], axis=1
        )
        res.append(lax.dot_general(lhs, up_ref[...], NT, preferred_element_type=F32))
    return jnp.where(low, res[0], res[1]).astype(BF16), jnp.where(low, res[2], 0.0).astype(BF16)


def half_kernel(own_ref, coef_ref, up_ref, part_ref, pown_ref):
    core = lax.axis_index("gz")

    def coef(row):
        return coef_ref[core, row : row + 1, :]

    for b in range(36):
        values = [own_ref[zp * 576 + b * 16 : zp * 576 + b * 16 + 16, :].astype(F32) for zp in range(3)]
        for s in range(SLOTS):
            part_ref[s, b * 16 : b * 16 + 16, :] = combine(values, coef, s * 12)
    pown_ref[0], pown_ref[1] = parents_of(own_ref, up_ref)


def forward_kernel(part_ref, pown_ref, other_ref, coef_ref, up_ref, fb_ref, fa_ref, fo_ref, po_ref, pq_ref, pp_s):
    core = lax.axis_index("gz")
    odd = lax.rem(lax.axis_index("gx"), 2)

    def coef(row):
        return coef_ref[core, row : row + 1, :]

    for face, base in ((fa_ref, 3 - 3 * odd), (fb_ref, 3 * odd)):
        for xx in range(3):
            for par in range(2):
                done = [[], [], []]
                for spot in range(3):
                    at = pl.multiple_of(base * 96 + (xx * 6 + 2 * spot + par) * 16, 16)
                    values = [other_ref[pl.ds(at + zp * 576, 16), :].astype(F32) for zp in range(3)]
                    for s in range(SLOTS):
                        val = part_ref[s, pl.ds(at, 16), :] + combine(values, coef, s * 12 + 6)
                        done[s].append(val)
                        fo_ref[s, base + xx, par, spot * 16 : spot * 16 + 16, :] = val.astype(BF16)
                outs_a, outs_b, rest = pack_three(*done)
                block = xx * 2 + par
                for spot in range(3):
                    at = (block * 3 + spot) * 16
                    face[at : at + 16, :] = outs_a[spot]
                    face[288 + at : 304 + at, :] = outs_b[spot]
                face[576 + block * 16 : 592 + block * 16, :] = rest
    pp_s[0:2] = pown_ref[...]
    pp_s[2], pp_s[3] = parents_of(other_ref, up_ref)
    firsts, seconds = [], []
    for x in range(3):
        for pos in range(3):
            at = (x * 3 + (0, 2, 1)[pos]) * 16
            values = [pp_s[v, at : at + 16, :].astype(F32) for v in range(4)]
            firsts.append(combine(values, coef, 72))
            seconds.append(combine(values, coef, 80))
            po_ref[x, pos * 16 : pos * 16 + 16, :] = firsts[-1].astype(BF16)
        pq_ref[x] = side_by_side(seconds[3 * x : 3 * x + 3])
    pack_parents((fa_ref, fb_ref), firsts, seconds)


def table_kernel(off_ref, zt_ref, far_ref, wl_ref, wp_ref, wq_ref, t3_s, w_s, a_s):
    core = lax.axis_index("gz")
    base = core * 80

    def spread(j, carry):
        for k in range(TERMS):
            at = pl.multiple_of(j * 104, 8) + 2 * k
            t3_s[pl.ds(at, 2), :] = far_ref[j, k].astype(F32)
        return carry

    lax.fori_loop(0, TERMS, spread, 0)
    t3_s[TERMS * 104 : 64 * 104, :] = jnp.zeros((15 * 104, 128), F32)
    for level, slots, start, out_ref in ((0, SLOTS, 0, wl_ref), (1, PSLOTS, 42, wp_ref)):
        ox = off_ref[level : level + 1, :]
        oy = off_ref[2 + level : 3 + level, :]
        oz = off_ref[4 + level : 5 + level, :]
        code = (ox + 3) * 7 + (oy + 3)
        chosen = lax.broadcasted_iota(jnp.int32, (56, 128), 0) == code
        for q in range(2 * slots):
            row = jnp.zeros((1, 128), F32)
            for d in range(7):
                row = jnp.where(oz == d - 3, zt_ref[base + start + q * 7 + d], row)
            full = jnp.where(chosen, row, 0.0)
            hi = full.astype(BF16).astype(F32)
            a_s[q * 56 : (q + 1) * 56, 0:128] = hi.astype(BF16)
            a_s[q * 56 : (q + 1) * 56, 128:256] = (full - hi).astype(BF16)
        count = slots * 56
        low = low_lanes(count)
        block = lax.broadcasted_iota(jnp.int32, (count, 128), 0)
        sign = -1.0
        both = low
        if level == 0:
            sign = jnp.where(block < 56, zt_ref[base + 70], -1.0)
        else:
            both = low | (block >= 56)
        turned = 168 if level == 0 else 56

        def two_terms(i, carry):
            k = 2 * i
            rhs = []
            for e in range(2):
                tk = t3_s[pl.ds(2 * (k + e) + level, 64, stride=104), :].astype(BF16)
                wide = jnp.concatenate([tk, tk], axis=1)
                rhs += [wide, wide]
            out = lax.dot_general(
                a_s[0 : 2 * count, :], jnp.concatenate(rhs, axis=0), NT, preferred_element_type=F32
            )
            for e in range(2):
                even = out[0:count, e * 128 : (e + 1) * 128]
                odd = out[count : 2 * count, e * 128 : (e + 1) * 128]
                w_s[pl.ds(k + e, count, stride=136), :] = jnp.where(both, even, odd)
                w_s[pl.ds(k + e + 64, turned, stride=136), :] = jnp.where(low, sign * odd, even)[0:turned]
            return carry

        lax.fori_loop(0, 25, two_terms, 0, unroll=5)
        inner = lax.broadcasted_iota(jnp.int32, (128, 128), 0)
        filled = (inner & 63) < TERMS

        def one_block(b, carry):
            val = w_s[pl.ds(pl.multiple_of(b * 136, 8), 128), :]
            out_ref[b] = jnp.where(filled, val, 0.0).astype(BF16)
            return carry

        lax.fori_loop(0, turned, one_block, 0, unroll=4)
    half = low_lanes(64)
    kept = lax.broadcasted_iota(jnp.int32, (64, 128), 0) < TERMS

    def one_step(xi, carry):
        def block_of(dy):
            if dy < -3 or dy > 3:
                return jnp.zeros((64, 128), F32)
            return w_s[pl.ds(pl.multiple_of((56 + xi * 7 + dy + 3) * 136, 8), 64), :]

        for i in range(4):
            d = 2 * i - 3
            for p in range(2):
                val = jnp.where(half, block_of(d + p), block_of(d + p - 1))
                wq_ref[xi, p * 64 : p * 64 + 64, i * 128 : (i + 1) * 128] = jnp.where(kept, val, 0.0).astype(BF16)
        return carry

    lax.fori_loop(0, 7, one_step, 0)


def weight_tiles(weights, s, diff, steps):
    d = 2 * diff + 3
    zero = jnp.zeros((128, 128), BF16)

    def weight(xi, dy):
        if dy < -3 or dy > 3:
            return zero
        return weights[s * 56 + xi * 7 + dy + 3]

    return jnp.concatenate(
        [
            jnp.concatenate([weight(xi, d + p), weight(xi, d + p - 1)], axis=1)
            for xi in steps
            for p in range(2)
        ],
        axis=0,
    )


def field_rows(field, s, steps, first, xs, rows):
    return jnp.concatenate(
        [field[s, first + xi : first + xi + xs, p].reshape(rows, 128) for xi in steps for p in range(2)],
        axis=1,
    )


def share_out(accs, s, xs, pairs, ys, put):
    spots = (ys + 1) // 2
    for pair in range(pairs):
        for o in range(2):
            yo = 2 * pair - 3 + o
            if yo >= ys + 3:
                continue
            val = None
            for diff in range(-3, 1):
                spot = pair + diff
                if 0 <= spot < spots:
                    part = accs[diff + 3][:, spot, :, o * 128 : (o + 1) * 128]
                    val = part if val is None else val + part
            for x in range(xs):
                put(s, x, yo, val[x])


SENT = ((0, 0, 2), (-1, 0, 1), (-2, 2, 3), (-3, 1, 3))
KEPT = ((0, 2, 3), (-1, 1, 3), (-2, 0, 2), (-3, 0, 1))


def spot_rows(field, s, steps, xs, span):
    rows = xs * 16 * (span[1] - span[0])
    cut = slice(span[0] * 16, span[1] * 16)
    return jnp.concatenate(
        [field[s, xi : xi + xs, p, cut].reshape(rows, 128) for xi in steps for p in range(2)], axis=1
    )


def near_kernel(fo_ref, wl_ref, acc_ref, fl_s):
    zero = jnp.zeros((SLOTS, 3, 2, 48, 128), BF16)
    fl_s[:, 0:3] = zero
    fl_s[:, 9:12] = zero
    fl_s[:, 3:9] = fo_ref[...]
    at = 0
    for s in range(SLOTS):
        for diff, lo, hi in SENT:
            lhs = spot_rows(fl_s, s, range(7), 6, (lo, hi))
            size = 96 * (hi - lo)
            acc_ref[at : at + size, :] = jnp.dot(
                lhs, weight_tiles(wl_ref, s, diff, range(7)), preferred_element_type=F32
            )
            at += size


def inner_kernel(fo_ref, fh_ref, edge_ref, wl_ref, own_ref, fl_s):
    fl_s[:, 0:3] = fh_ref[:, 0:3]
    fl_s[:, 9:12] = fh_ref[:, 3:6]
    fl_s[:, 3:9] = fo_ref[...]
    for s in range(SLOTS):
        accs = {}
        for diff, lo, hi in KEPT:
            lhs = spot_rows(fl_s, s, range(7), 6, (lo, hi))
            acc = jnp.dot(lhs, weight_tiles(wl_ref, s, diff, range(7)), preferred_element_type=F32)
            acc = acc.reshape(6, hi - lo, 16, 256)
            for spot in range(lo, hi):
                accs[diff, spot] = acc[:, spot - lo]
        for pair in (2, 3):
            val = accs[-pair, 0] + accs[1 - pair, 1] + accs[2 - pair, 2]
            for x in range(6):
                for o in range(2):
                    at = ((s * 6 + x) * 6 + 2 * pair - 3 + o) * 16
                    own_ref[at : at + 16, :] = val[x, :, o * 128 : (o + 1) * 128]
        for x in range(6):
            at = (s * 6 + x) * 96
            edge = (s * 6 + x) * 32
            own_ref[at : at + 16, :] = edge_ref[edge : edge + 16, :]
            own_ref[at + 80 : at + 96, :] = edge_ref[edge + 16 : edge + 32, :]


def far_kernel(
    b_ref, a_ref, acc_ref, po_ref, pq_ref, wl_ref, wp_ref, wq_ref,
    sb_ref, sa_ref, fh_ref, edge_ref, pown_ref, fl_s, fp_s, fq_s, ex_s, px_s
):
    xodd = lax.rem(lax.axis_index("gx"), 2)
    yodd = lax.rem(lax.axis_index("gy"), 2)
    fl_s[:, 3:6] = jnp.zeros((SLOTS, 3, 2, 48, 128), BF16)
    fp_s[0, :, 1, 16:32] = jnp.zeros((9, 16, 128), BF16)
    part = po_ref[...]
    fp_s[0, 3:6, 0] = part[:, 0:32]
    fp_s[0, 3:6, 1, 0:16] = part[:, 32:48]
    fq_s[3:6] = pq_ref[...]
    for ref, far_side in ((a_ref, 1 - xodd), (b_ref, xodd)):
        for x in range(3):
            for par in range(2):
                block = x * 2 + par
                rest = ref[576 + block * 16 : 592 + block * 16, :].astype(F32)
                for spot in range(3):
                    at = (block * 3 + spot) * 16
                    one = ref[at : at + 16, :]
                    two = ref[288 + at : 304 + at, :]
                    three = unpack_third(one.astype(F32), two.astype(F32), rest, spot)
                    for s, val in enumerate((one, two, three.astype(BF16))):
                        fl_s[s, far_side * 6 + x, par, spot * 16 : spot * 16 + 16, :] = val
                        fh_ref[s, far_side * 3 + x, par, spot * 16 : spot * 16 + 16, :] = val
            for pos in range(3):
                b = x * 3 + pos
                at = (pos % 2) * 16
                fp_s[0, far_side * 6 + x, pos // 2, at : at + 16] = ref[672 + b * 16 : 688 + b * 16, :]
            fq_s[far_side * 6 + x] = side_by_side([unpack_second(ref, x * 3 + pos) for pos in range(3)])

    def parent_put(s, x, yo, val):
        if 0 <= yo < 3:
            at = ((s * 3 + x) * 3 + yo) * 16
            pown_ref[at : at + 16, :] = val
        else:
            px_s[0 if yo < 0 else 1, s, x * 3 + (yo + 3 if yo < 0 else yo - 3)] = val

    row = 0
    for s in range(SLOTS):
        accs = {}
        for diff, lo, hi in SENT:
            half = 48 * (hi - lo)
            for i, steps in enumerate((range(3), range(4, 7))):
                lhs = spot_rows(fl_s, s, steps, 3, (lo, hi))
                acc = acc_ref[row : row + half, :] + jnp.dot(
                    lhs, weight_tiles(wl_ref, s, diff, steps), preferred_element_type=F32
                )
                row += half
                acc = acc.reshape(3, hi - lo, 16, 256)
                for spot in range(lo, hi):
                    for x in range(3):
                        accs[diff, spot, 3 * i + x] = acc[x, spot - lo]
        for x in range(6):
            low = accs[0, 0, x]
            low_next = accs[-1, 0, x] + accs[0, 1, x]
            high_next = accs[-3, 1, x] + accs[-2, 2, x]
            high = accs[-3, 2, x]
            ex_s[0, s, x, 0] = low[:, 0:128]
            ex_s[0, s, x, 1] = low[:, 128:256]
            ex_s[0, s, x, 2] = low_next[:, 0:128]
            ex_s[1, s, x, 0] = high_next[:, 128:256]
            ex_s[1, s, x, 1] = high[:, 0:128]
            ex_s[1, s, x, 2] = high[:, 128:256]
            edge = (s * 6 + x) * 32
            edge_ref[edge : edge + 16, :] = low_next[:, 128:256]
            edge_ref[edge + 16 : edge + 32, :] = high_next[:, 0:128]
    lhs = field_rows(fp_s, 0, range(7), 0, 3, 96)
    accs = [
        jnp.dot(lhs, weight_tiles(wp_ref, 0, diff, range(7)), preferred_element_type=F32).reshape(3, 2, 16, 256)
        for diff in range(-3, 1)
    ]
    share_out(accs, 0, 3, 5, 3, parent_put)
    lhs = jnp.concatenate([fq_s[xi : xi + 3].reshape(96, 128) for xi in range(7)], axis=1)
    acc = jnp.dot(lhs, wq_ref[...].reshape(896, 512), preferred_element_type=F32).reshape(3, 2, 16, 512)
    for pair in range(5):
        val = None
        for diff in range(-3, 1):
            spot = pair + diff
            if 0 <= spot < 2:
                piece = acc[:, spot, :, (diff + 3) * 128 : (diff + 4) * 128]
                val = piece if val is None else val + piece
        for x in range(3):
            parent_put(1, x, 2 * pair - 3, val[x])
            if pair < 4:
                parent_put(1, x, 2 * pair - 2, pltpu.roll(val[x], 64, 1))
    for side, ref in ((1 - yodd, sa_ref), (yodd, sb_ref)):
        for x in range(6):
            outs_a, outs_b, rest = pack_three(
                *[[ex_s[side, s, x, i] for i in range(3)] for s in range(SLOTS)]
            )
            for i in range(3):
                at = (x * 3 + i) * 16
                ref[at : at + 16, :] = outs_a[i]
                ref[288 + at : 304 + at, :] = outs_b[i]
            ref[576 + x * 16 : 592 + x * 16, :] = rest
        pack_parents((ref,), *[[px_s[side, s, b] for b in range(9)] for s in range(PSLOTS)])


def join_kernel(own_ref, pown_ref, b_ref, a_ref, full_ref, zs_ref):
    yodd = lax.rem(lax.axis_index("gy"), 2)
    for ref, upper in ((a_ref, 1 - yodd), (b_ref, yodd)):
        for x in range(6):
            rest = ref[576 + x * 16 : 592 + x * 16, :].astype(F32)
            for i in range(3):
                at = (x * 3 + i) * 16
                one = ref[at : at + 16, :].astype(F32)
                two = ref[288 + at : 304 + at, :].astype(F32)
                three = unpack_third(one, two, rest, i)
                for s, val in enumerate((one, two, three)):
                    row = pl.multiple_of(((s * 6 + x) * 6 + i) * 16 + upper * 48, 16)
                    total = own_ref[pl.ds(row, 16), :] + val
                    full_ref[pl.ds(row, 16), :] = total
                    zs_ref[pl.ds(row, 16), :] = total.astype(BF16)
    for b in range(9):
        for s in range(PSLOTS):
            row = 1728 + (s * 9 + b) * 16
            total = pown_ref[row - 1728 : row - 1712, :]
            for ref in (a_ref, b_ref):
                if s == 0:
                    total = total + ref[672 + b * 16 : 688 + b * 16, :].astype(F32)
                else:
                    total = total + unpack_second(ref, b)
            full_ref[row : row + 16, :] = total
            zs_ref[row : row + 16, :] = total.astype(BF16)


def back_kernel(own_ref, coef_ref, part_ref, ppart_ref):
    core = lax.axis_index("gz")

    def coef(row):
        return coef_ref[core, row : row + 1, :]

    for i in range(9):
        at = 1728 + i * 16
        values = [own_ref[at + s * 144 : at + s * 144 + 16, :] for s in range(PSLOTS)]
        for p in range(2):
            ppart_ref[p, i * 16 : (i + 1) * 16, :] = combine(values, coef, 88 + p * 8)
    for b in range(36):
        values = [own_ref[s * 576 + b * 16 : s * 576 + b * 16 + 16, :] for s in range(SLOTS)]
        for zp in range(3):
            part_ref[zp, b * 16 : b * 16 + 16, :] = combine(values, coef, 36 + zp * 12)


def atoms_kernel(part_ref, ppart_ref, other_ref, coef_ref, one_ref, h_ref, down_ref, out_ref, pf_s, lift_s, l_s, l2_s):
    core = lax.axis_index("gz")

    def coef(row):
        return coef_ref[core, row : row + 1, :]

    for i in range(9):
        at = 1728 + i * 16
        values = [other_ref[at + s * 144 : at + s * 144 + 16, :].astype(F32) for s in range(PSLOTS)]
        for p in range(2):
            total = ppart_ref[p, i * 16 : (i + 1) * 16, :] + combine(values, coef, 92 + p * 8)
            hi = total.astype(BF16)
            pf_s[p, i * 16 : (i + 1) * 16, 0:128] = hi
            pf_s[p, i * 16 : (i + 1) * 16, 128:256] = (total - hi.astype(F32)).astype(BF16)
    for k in range(3):
        table = jnp.concatenate([down_ref[k % 2], down_ref[k % 2]], axis=1)
        lift_s[k] = lax.dot_general(pf_s[k // 2], table, NT, preferred_element_type=F32)
    for x in range(6):
        for y in range(6):
            at = (x * 6 + y) * 16
            values = [other_ref[s * 576 + at : s * 576 + at + 16, :].astype(F32) for s in range(SLOTS)]
            par = ((x // 2) * 3 + y // 2) * 16
            lane = ((x % 2) * 2 + y % 2) * 128
            for zp in range(3):
                l_s[zp, at : at + 16, :] = (
                    part_ref[zp, at : at + 16, :]
                    + combine(values, coef, 42 + zp * 12)
                    + lift_s[zp, par : par + 16, lane : lane + 128]
                )
    low = low_lanes(40)
    for zp in range(3):
        l_s[zp, 576:640, :] = jnp.zeros((64, 128), F32)
        for cp in range(8):
            a = l_s[zp, pl.ds(2 * cp, 40, stride=16), :]
            b = l_s[zp, pl.ds(2 * cp + 1, 40, stride=16), :]
            first = jnp.where(low, a, pltpu.roll(b, 64, 1))
            second = jnp.where(low, pltpu.roll(a, 64, 1), b)
            for z, val in ((2 * zp, first), (2 * zp + 1, second)):
                l2_s[z * 40 : (z + 1) * 40, cp * 128 : (cp + 1) * 128] = val
    l2_s[240:256, :] = jnp.zeros((16, 1024), F32)
    rows = l2_s[...].T.reshape(CH, 64, 256)[:, 0:56].reshape(CH * 56, 256).astype(BF16)
    for i in range(8):
        spread = jnp.dot(rows, one_ref[:, i * 256 : (i + 1) * 256], preferred_element_type=F32)
        spread = spread.reshape(CH, 56, 256) * h_ref[0:56, i * 256 : (i + 1) * 256][None]
        out_ref[0, 0, 0, :, i * 256 : (i + 1) * 256] = jnp.sum(spread, axis=1)


def call(kernel, outs, scratch, limit, flops, moved, in_specs=None):
    placed = {} if in_specs is None else {"in_specs": in_specs}
    return pl.pallas_call(
        kernel,
        out_shape=outs,
        **placed,
        scratch_shapes=scratch,
        compiler_params=pltpu.CompilerParams(vmem_limit_bytes=limit * MIB),
        cost_estimate=pl.CostEstimate(flops=flops, bytes_accessed=moved, transcendentals=0),
    )


def shape(dims, dtype):
    return jax.ShapeDtypeStruct(dims, dtype)


def swaps(axis):
    count = lax.axis_size(axis)
    inner = [(i, i ^ 1) for i in range(count)]
    outer = [(i, (i + (1 if i % 2 else -1)) % count) for i in range(count)]
    return inner, outer


def far_weights(off, table, far):
    vmem = pl.BlockSpec(memory_space=pltpu.VMEM)
    return call(
        table_kernel,
        (shape((SLOTS * 56, 128, 128), BF16), shape((56, 128, 128), BF16), shape((7, 128, 512), BF16)),
        [
            pltpu.VMEM((64 * 104, 128), F32),
            pltpu.VMEM((SLOTS * 56 * 136, 128), F32),
            pltpu.VMEM((SLOTS * 112, 256), BF16),
        ],
        24,
        2 * 49 * 5 * 112 * 256 * 256,
        10 * MIB,
        [vmem, pl.BlockSpec(memory_space=pltpu.SMEM), vmem],
    )(off, table, far)


def per_device(charges, positions, atom_cells, offsets, far_tables, upward_tables, downward_tables):
    up = jnp.pad(upward_tables.transpose(1, 0, 2), ((0, 15), (0, 0), (0, 15))).reshape(64, 512)
    up = jnp.concatenate([up, up], axis=0)
    down = jnp.pad(downward_tables, ((0, 0), (0, 15), (0, 15))).reshape(512, 64)
    blank = jnp.zeros_like(down)
    down = jnp.stack(
        [jnp.concatenate([down, blank], axis=1), jnp.concatenate([blank, down], axis=1)], axis=0
    )
    off = offsets.transpose(2, 0, 1).reshape(6, NOFF)
    far = far_tables.transpose(1, 2, 0, 3)
    coefs = jnp.asarray(COEFS)
    ztable = jnp.asarray(ZTABLE)
    cells = atom_cells.reshape(16, 128)
    swap = [(0, 1), (1, 0)]

    positions = pltpu.with_memory_space_constraint(positions.reshape(48, 128), pltpu.HBM)
    cells = pltpu.with_memory_space_constraint(cells, pltpu.HBM)
    leaf_z = call(
        poles_kernel,
        shape((1728, 128), BF16),
        [
            pltpu.VMEM((64, 2048), F32),
            pltpu.VMEM((256, 2048), BF16),
            pltpu.VMEM((16, 2048), BF16),
            pltpu.VMEM((48, 128), F32),
            pltpu.VMEM((16, 128), jnp.int32),
            pltpu.VMEM((1024, 128), F32),
            pltpu.VMEM((16, 2048), F32),
            pltpu.VMEM((1024, 4096), BF16),
            pltpu.VMEM((3, 640, 128), F32),
            pltpu.SemaphoreType.DMA((3,)),
        ],
        20,
        2 * 2 * 256 * 2048 * 1024,
        2 * MIB,
        [pl.BlockSpec(memory_space=pltpu.HBM)] * 3,
    )(pltpu.with_memory_space_constraint(charges, pltpu.HBM), positions, cells)
    leaf_other = lax.ppermute(leaf_z, "gz", swap)
    part, pown = call(
        half_kernel,
        (shape((SLOTS, 576, 128), F32), shape((2, 144, 128), BF16)),
        [],
        8,
        1 << 27,
        2 * MIB,
    )(leaf_z, coefs, up)
    face = shape((848, 128), BF16)
    fb, fa, fo, po, pq = call(
        forward_kernel,
        (face, face, shape((SLOTS, 6, 2, 48, 128), BF16), shape((3, 48, 128), BF16), shape((3, 32, 128), BF16)),
        [pltpu.VMEM((4, 144, 128), BF16)],
        8,
        1 << 28,
        2 * MIB,
    )(part, pown, leaf_other, coefs, up)
    inner, outer = swaps("gx")
    fa = lax.ppermute(fa, "gx", inner)
    fb = lax.ppermute(fb, "gx", outer)
    fo, off = lax.optimization_barrier((fo, off))
    wl, wp, wq = far_weights(off, ztable, far)
    near = call(
        near_kernel,
        shape((SLOTS * 576, 256), F32),
        [pltpu.VMEM((SLOTS, 12, 2, 48, 128), BF16)],
        16,
        2 * 144 * 1792 * 256 * 12,
        8 * MIB,
    )(fo, wl)
    sb, sa, fh, edge, pown = call(
        far_kernel,
        (
            face,
            face,
            shape((SLOTS, 6, 2, 48, 128), BF16),
            shape((SLOTS * 192, 128), F32),
            shape((288, 128), F32),
        ),
        [
            pltpu.VMEM((SLOTS, 9, 2, 48, 128), BF16),
            pltpu.VMEM((1, 9, 2, 32, 128), BF16),
            pltpu.VMEM((9, 32, 128), BF16),
            pltpu.VMEM((2, SLOTS, 6, 3, 16, 128), F32),
            pltpu.VMEM((2, PSLOTS, 9, 16, 128), F32),
        ],
        16,
        2 * 288 * 1792 * 256 * 8,
        14 * MIB,
    )(fb, fa, near, po, pq, wl, wp, wq)
    inner, outer = swaps("gy")
    sa = lax.ppermute(sa, "gy", inner)
    sb = lax.ppermute(sb, "gy", outer)
    edge, positions, cells = lax.optimization_barrier((edge, positions, cells))
    own = call(
        inner_kernel,
        shape((1728, 128), F32),
        [pltpu.VMEM((SLOTS, 12, 2, 48, 128), BF16)],
        16,
        2 * 144 * 1792 * 256 * 12,
        8 * MIB,
    )(fo, fh, edge, wl)
    harm, one = call(
        atom_terms_kernel,
        (shape((64, 2048), F32), shape((256, 2048), BF16)),
        [pltpu.VMEM((1024, 128), F32)],
        8,
        1 << 24,
        2 * MIB,
    )(positions, cells)
    own, harm, one = lax.optimization_barrier((own, harm, one))
    full, zsend = call(
        join_kernel, (shape((2016, 128), F32), shape((2016, 128), BF16)), [], 8, 1 << 20, 3 * MIB
    )(own, pown, sb, sa)
    zrecv = lax.ppermute(zsend, "gz", swap)
    part, ppart = call(
        back_kernel,
        (shape((SLOTS, 576, 128), F32), shape((2, 144, 128), F32)),
        [],
        8,
        1 << 24,
        2 * MIB,
    )(full, coefs)
    potential = call(
        atoms_kernel,
        shape((1, 1, 1, CH, 2048), F32),
        [
            pltpu.VMEM((2, 144, 256), BF16),
            pltpu.VMEM((3, 144, 512), F32),
            pltpu.VMEM((3, 640, 128), F32),
            pltpu.VMEM((256, 1024), F32),
        ],
        16,
        2 * 2 * 256 * 2048 * 1024,
        2 * MIB,
    )(part, ppart, zrecv, coefs, one, harm, down)
    return potential


def solution(mesh):
    placed = (
        P("gx", "gy", "gz", None, None),
        P("gx", "gy", "gz", None, None),
        P("gx", "gy", "gz", None),
        P(),
        P(),
        P(),
        P(),
    )
    return jax.shard_map(
        per_device,
        mesh=mesh,
        in_specs=placed,
        out_specs=P("gx", "gy", "gz", None, None),
        check_vma=False,
    )
```
